32 devices in a mesh: row: 8 (over y, x, core), col: 4 (over z).
Axes of the slice: x: 2, y: 2, z: 4, core: 2. Of those that a mesh axis runs over, the one named last changes fastest.
Arguments:
- embeddings: bfloat16 [16384, 1024], P('row'), may hold values from -6 to 6
- vectors: bfloat16 [64, 16384], P(None, ('row', 'col')), may hold values from -6 to 6
- block_pairs: int32 [992, 2], replicated, may hold values from 0 to 31, as said below
Outputs:
- new_basis: float32 [64, 16384], P(None, ('row', 'col'))
The draws below stay inside these ranges and needn't reach their ends.
Inputs may be any that keep to these rules, and one draw needn't show every extreme that they name: `block_pairs`: no pair is listed twice, no pair has equal blocks, and every block occurs as a row block at least once.
All inputs are finite; a program needn't handle non-finite values.
Results may differ from the reference program's by a relative error of at most 0.0032.
Values may be sent and summed in bfloat16 or wider, within the bound.
A program may use at most 128 MiB of HBM per device.

```python
import math
import jax
import jax.numpy as jnp
from jax import lax

BLOCK = 512
WIDTH = 1024
EIGS = 64
NBLOCKS = 32
NROWS = 16384
NPAIRS = 992


def draw_block_pairs(key, part):
    total = NBLOCKS * NBLOCKS
    index = jnp.arange(total, dtype=jnp.int32)
    row_of = index // NBLOCKS
    col_of = index % NBLOCKS
    level = jnp.arange(NBLOCKS, dtype=jnp.int32) * 4 // NBLOCKS
    noise = jax.random.randint(key, (total,), 0, 4096, dtype=jnp.int32)
    score = noise * (1 + level[row_of] + level[col_of])
    forced = (col_of == (row_of + 1) % NBLOCKS) | (col_of == (row_of + NBLOCKS // 2) % NBLOCKS)
    score = jnp.where(forced, 65535, score)
    score = jnp.where(row_of == col_of, -1, score)
    keyed = score * total + index
    chosen = lax.top_k(keyed, NPAIRS)[1]
    return jnp.stack([row_of[chosen], col_of[chosen]], axis=1).astype(jnp.int32)


def shard_levels(own_key, shape, shards, low, high):
    factor_of, own = 1.0, jax.random.fold_in(own_key, 6)
    for axis_at, parts in shards:
        heights = jnp.exp(jax.random.uniform(jax.random.fold_in(own, axis_at), (parts,), jnp.float32, low / len(shards), high / len(shards)))
        factor_of = factor_of * jnp.repeat(heights, shape[axis_at] // parts).reshape([-1 if axis == axis_at else 1 for axis in range(len(shape))])
    return factor_of


def gaussian(stream_key, extent, spread, limit, pieces=(), held_as=jnp.bfloat16):
    factor_of = shard_levels(stream_key, extent, pieces, -0.22, 0.18) if pieces else 1.0
    result = jax.random.normal(stream_key, extent, jnp.float32) * spread * factor_of
    return jnp.minimum(jnp.maximum(result, -limit), limit).astype(held_as)


def setup_inputs(seed: int = 0) -> dict:
    key_list = jax.random.split(jax.random.key(seed), 4)
    return {
        "embeddings": gaussian(key_list[0], (NROWS, WIDTH), 1.0, 6.0, ((0, 8),)),
        "vectors": gaussian(key_list[1], (EIGS, NROWS), 1.0, 6.0, ((1, 32),)),
        "block_pairs": draw_block_pairs(jax.random.fold_in(key_list[3], 71), 0),
    }


def reference(embeddings, vectors, block_pairs):
    row_norms = lax.rsqrt(lax.optimization_barrier(jnp.mean(jnp.square(embeddings.astype(jnp.float32)), axis=1)) + 1e-06)

    def one_tile(running, pair_now):
        partial_sums, degree = running
        row_start = (pair_now[0] * BLOCK).astype(jnp.int32)
        col_start = (pair_now[1] * BLOCK).astype(jnp.int32)
        rows_x = lax.dynamic_slice_in_dim(embeddings, row_start, BLOCK, 0)
        cols_x = lax.dynamic_slice_in_dim(embeddings, col_start, BLOCK, 0)
        norm_rows = lax.dynamic_slice_in_dim(row_norms, row_start, BLOCK, 0)
        norm_cols = lax.dynamic_slice_in_dim(row_norms, col_start, BLOCK, 0)
        scores = jnp.dot(rows_x.astype(jnp.float32), cols_x.T.astype(jnp.float32), preferred_element_type=jnp.float32)
        affinity = jnp.exp(scores * norm_rows[:, None] * norm_cols[None, :] / math.sqrt(WIDTH))
        rounded = affinity.astype(jnp.bfloat16)
        cols_v = lax.dynamic_slice_in_dim(vectors, col_start, BLOCK, 1)
        contrib = jnp.dot(cols_v.astype(jnp.float32), rounded.T.astype(jnp.float32), preferred_element_type=jnp.float32)
        old_sums = lax.dynamic_slice_in_dim(partial_sums, row_start, BLOCK, 1)
        partial_sums = lax.dynamic_update_slice_in_dim(partial_sums, old_sums + contrib, row_start, 1)
        old_degree = lax.dynamic_slice_in_dim(degree, row_start, BLOCK, 0)
        degree = lax.dynamic_update_slice_in_dim(degree, old_degree + lax.optimization_barrier(jnp.sum(affinity, axis=1)), row_start, 0)
        return ((partial_sums, degree), None)
    start_sums = jnp.zeros((EIGS, NROWS), jnp.float32)
    start_degree = jnp.zeros((NROWS,), jnp.float32)
    (partial_sums, degree), unused = lax.scan(one_tile, (start_sums, start_degree), block_pairs)
    smoothed = partial_sums / degree[None, :]
    gram_matrix = jnp.dot(smoothed.astype(jnp.float32), smoothed.T.astype(jnp.float32), precision=lax.Precision.HIGHEST, preferred_element_type=jnp.float32) / NROWS
    factor = jnp.linalg.cholesky(gram_matrix)
    return lax.linalg.triangular_solve(factor, smoothed, left_side=True, lower=True)
```

```python
import functools
import math

import jax
import jax.numpy as jnp
from jax import lax
from jax.experimental import pallas as pl
from jax.experimental.pallas import tpu as pltpu
from jax.sharding import PartitionSpec as P


def inverse_norms(blocks):
    return lax.rsqrt(jnp.mean(jnp.square(blocks.astype(jnp.float32)), axis=-1) + 1e-06)


def tile_terms(rows_x, cols_x, norm_rows, norm_cols, cols_v, feature_width):
    scores = jnp.dot(rows_x, cols_x.T, preferred_element_type=jnp.float32)
    affinity = jnp.exp(scores * norm_rows[:, None] * norm_cols[None, :] / math.sqrt(feature_width))
    rounded = affinity.astype(jnp.bfloat16)
    contrib = jnp.dot(cols_v, rounded.T, preferred_element_type=jnp.float32)
    return (contrib, jnp.sum(affinity, axis=1))


def tile_mask(block_pairs, near_column, col_count, row_count, here_row, here_col):
    near_ids = block_pairs[:, near_column]
    far_ids = block_pairs[:, 1 - near_column]
    member = (near_ids // col_count == here_row) & (far_ids % col_count == here_col)
    near_hot = ((near_ids % col_count)[:, None] == jnp.arange(col_count)[None, :]) & member[:, None]
    far_hot = (far_ids // col_count)[:, None] == jnp.arange(row_count)[None, :]
    return jnp.dot(
        near_hot.astype(jnp.float32).T,
        far_hot.astype(jnp.float32),
        preferred_element_type=jnp.float32,
    )


def add_block(running, contrib, row_totals, column_start, block_rows):
    sums_now, degree_now = running
    old_sums = lax.dynamic_slice_in_dim(sums_now, column_start, block_rows, 1)
    sums_now = lax.dynamic_update_slice_in_dim(sums_now, old_sums + contrib, column_start, 1)
    old_degree = lax.dynamic_slice_in_dim(degree_now, column_start, block_rows, 1)
    degree_now = lax.dynamic_update_slice_in_dim(
        degree_now, old_degree + row_totals[None, :], column_start, 1
    )
    return (sums_now, degree_now)


def per_device(embeddings, vectors, block_pairs):
    col_count = lax.axis_size("col")
    row_count = lax.axis_size("row")
    here_row = lax.axis_index("row")
    here_col = lax.axis_index("col")
    eig_count, block_rows = vectors.shape
    feature_width = embeddings.shape[1]
    near_blocks = embeddings.reshape(col_count, block_rows, feature_width)
    near_norms = inverse_norms(near_blocks)
    own_block = lax.dynamic_slice_in_dim(near_blocks, here_col, 1, 0)
    present = tile_mask(block_pairs, 0, col_count, row_count, here_row, here_col)
    start_sums = jnp.zeros((eig_count, col_count * block_rows), jnp.float32)
    start_degree = jnp.zeros((1, col_count * block_rows), jnp.float32)
    far_x = lax.all_gather(own_block, "row", axis=0, tiled=True)
    far_v = lax.all_gather(vectors[None], "row", axis=0, tiled=True)
    far_norms = inverse_norms(far_x)
    piece_blocks = far_x.shape[0]

    def visit(position, current):
        far_index = position // col_count
        near_index = position % col_count

        def compute(totals):
            contrib, row_totals = tile_terms(
                near_blocks[near_index],
                far_x[far_index],
                near_norms[near_index],
                far_norms[far_index],
                far_v[far_index],
                feature_width,
            )
            return add_block(totals, contrib, row_totals, near_index * block_rows, block_rows)

        return lax.cond(
            present[near_index, far_index] > 0.5, compute, lambda totals: totals, current
        )

    partial_sums, degree = lax.fori_loop(
        0, piece_blocks * col_count, visit, (start_sums, start_degree)
    )
    owned_sums, owned_degree = (
        lax.psum_scatter(partial_sums, "col", scatter_dimension=1, tiled=True),
        lax.psum_scatter(degree, "col", scatter_dimension=1, tiled=True),
    )
    smoothed = owned_sums / owned_degree
    total_rows = block_rows * col_count * row_count
    local_gram = jnp.dot(
        smoothed, smoothed.T, precision=lax.Precision.HIGHEST, preferred_element_type=jnp.float32
    )
    gram_matrix = lax.psum(local_gram, ("row", "col")) / total_rows
    factor = jnp.linalg.cholesky(gram_matrix)
    return lax.linalg.triangular_solve(factor, smoothed, left_side=True, lower=True)


UNITS = 16
FIRST_SENDS = ((0, 4, 2), (1, 5, 4), (0, 2, 1), (1, 3, 1), (1, 8, 2), (0, 9, 4))
RELAYS = {
    4: ((4, 12, 4), (5, 13, 2), (4, 6, 1), (5, 7, 1)),
    8: ((8, 10, 1), (9, 11, 1)),
    12: ((12, 14, 1), (13, 15, 1)),
}


def across(row, bits):
    if bits & 1:
        row = row + 1 - 2 * (row % 2)
    if bits & 2:
        row = row + 2 - 4 * ((row // 2) % 2)
    if bits & 4:
        row = row + 4 - 8 * ((row // 4) % 2)
    return row


def whole_kernel(
    total_rows,
    x_hbm,
    v_ref,
    out_ref,
    own_x,
    far_x,
    far_v,
    own_norm,
    acc,
    parts,
    plane_gram,
    depth_gram,
    own_sem,
    x_send,
    x_recv,
    v_send,
    v_recv,
    part_send,
    part_recv,
    plane_send,
    plane_recv,
    depth_send,
    depth_recv,
):
    row = lax.axis_index("row")
    col = lax.axis_index("col")
    row_count = plane_gram.shape[0]
    col_count, padded, block_rows = acc.shape
    eig_count = v_ref.shape[0]
    half = block_rows // 2
    width = own_x.shape[1]
    mesh_ids = pl.DeviceIdType.MESH

    load = pltpu.make_async_copy(x_hbm, own_x, own_sem)
    load.start()

    barrier = pltpu.get_barrier_semaphore()
    for bits in range(1, row_count):
        pl.semaphore_signal(barrier, inc=1, device_id=(across(row, bits), col), device_id_type=mesh_ids)
    for step in range(1, col_count):
        pl.semaphore_signal(barrier, inc=1, device_id=(row, (col + step) % col_count), device_id_type=mesh_ids)
    pl.semaphore_wait(barrier, row_count + col_count - 2)

    def unit_copies(source, target, bits):
        if source < 2:
            start = pl.multiple_of(col * block_rows + source * half, half)
            x_src = x_hbm.at[pl.ds(start, half), :]
            v_src = v_ref.at[:, pl.ds(source * half, half)]
        else:
            x_src = far_x.at[source]
            v_src = far_v.at[source]
        partner = (across(row, bits), col)
        return (
            pltpu.make_async_remote_copy(
                src_ref=v_src, dst_ref=far_v.at[target], send_sem=v_send.at[target],
                recv_sem=v_recv.at[target], device_id=partner, device_id_type=mesh_ids,
            ),
            pltpu.make_async_remote_copy(
                src_ref=x_src, dst_ref=far_x.at[target], send_sem=x_send.at[target],
                recv_sem=x_recv.at[target], device_id=partner, device_id_type=mesh_ids,
            ),
        )

    def start_unit(item):
        for copy in unit_copies(*item):
            copy.start()

    def wait_unit(target):
        pltpu.make_async_copy(far_v.at[target], far_v.at[target], v_recv.at[target]).wait()
        pltpu.make_async_copy(far_x.at[target], far_x.at[target], x_recv.at[target]).wait()

    for item in FIRST_SENDS:
        start_unit(item)

    load.wait()
    far_v[0] = v_ref[:, :half]
    far_v[1] = v_ref[:, half:]
    for part in range(2):
        start = pl.multiple_of(col * block_rows + part * half, half)
        far_x[part] = own_x[pl.ds(start, half), :]
    acc[...] = jnp.zeros_like(acc)

    @pl.loop(0, col_count)
    def _(near):
        rows = own_x[pl.ds(pl.multiple_of(near * block_rows, block_rows), block_rows), :].astype(jnp.float32)
        mean = jnp.sum(rows * rows, axis=1, keepdims=True) * (1.0 / width)
        norm = lax.rsqrt(mean + 1e-06)
        turned = jnp.broadcast_to(norm, (block_rows, 128)).T
        own_norm[near] = turned[0:8, :]

    scale = 1.4426950408889634 / math.sqrt(width)

    @pl.loop(0, UNITS)
    def _(unit):
        @pl.when(unit == 2)
        def _():
            acc[col] = jnp.zeros((padded, block_rows), jnp.float32)

        for first, items in RELAYS.items():
            @pl.when(unit == first)
            def _(first=first, items=items):
                wait_unit(first)
                wait_unit(first + 1)
                for item in items:
                    start_unit(item)

        for alone in (2, 3, 6, 7, 10, 11, 14, 15):
            @pl.when(unit == alone)
            def _(alone=alone):
                wait_unit(alone)

        cols = far_x[unit]
        wide = cols.astype(jnp.float32)
        mean = jnp.sum(wide * wide, axis=1, keepdims=True) * (1.0 / width)
        col_norm = lax.rsqrt(mean + 1e-06) * scale
        cols_v = far_v[unit]
        for near in range(col_count):
            scores = lax.dot_general(
                cols, own_x[near * block_rows : (near + 1) * block_rows, :],
                (((1,), (1,)), ((), ())), preferred_element_type=jnp.float32,
            )
            affinity = jnp.exp2(scores * own_norm[near, 0:1, :] * col_norm)
            acc[near, eig_count:, :] += jnp.sum(affinity.reshape(half // 8, 8, block_rows), axis=0)
            acc[near, :eig_count, :] += jnp.dot(
                cols_v, affinity.astype(jnp.bfloat16), preferred_element_type=jnp.float32
            )

    def part_copy(step):
        target = (col + step) % col_count
        return pltpu.make_async_remote_copy(
            src_ref=acc.at[target], dst_ref=parts.at[step - 1], send_sem=part_send.at[step - 1],
            recv_sem=part_recv.at[step - 1], device_id=(row, target), device_id_type=mesh_ids,
        )

    for step in range(1, col_count):
        part_copy(step).start()
    total = acc[col]
    for step in range(1, col_count):
        part_copy(step).wait_recv()
        total = total + parts[step - 1]
    degree = jnp.sum(total[eig_count:, :], axis=0, keepdims=True)
    smoothed = total[:eig_count, :] / degree

    def gram_sum(gram, held, me, partners, send_sem, recv_sem):
        held[me] = gram
        copies = []
        for at, partner in enumerate(partners):
            copies.append(
                pltpu.make_async_remote_copy(
                    src_ref=held.at[me], dst_ref=held.at[me], send_sem=send_sem.at[at],
                    recv_sem=recv_sem.at[at], device_id=partner, device_id_type=mesh_ids,
                )
            )
        for copy in copies:
            copy.start()
        for copy in copies:
            copy.wait()
        return jnp.sum(held[...], axis=0)

    gram = lax.dot_general(
        smoothed, smoothed, (((1,), (1,)), ((), ())),
        precision=lax.Precision.HIGHEST, preferred_element_type=jnp.float32,
    )
    gram = gram_sum(
        gram, plane_gram, row, [(across(row, bits), col) for bits in range(1, row_count)],
        plane_send, plane_recv,
    )
    gram = gram_sum(
        gram, depth_gram, col, [(row, (col + step) % col_count) for step in range(1, col_count)],
        depth_send, depth_recv,
    )
    gram = gram / total_rows

    down = lax.broadcasted_iota(jnp.int32, (eig_count, 1), 0)
    at_row = lax.broadcasted_iota(jnp.int32, (eig_count, eig_count), 0)
    at_col = lax.broadcasted_iota(jnp.int32, (eig_count, eig_count), 1)
    diagonal = at_row == at_col
    work = jnp.concatenate([diagonal.astype(jnp.float32), gram], axis=1)
    for step in range(eig_count - 1):
        at = eig_count + step
        pivot = work[step : step + 1, :]
        ratio = work[:, at : at + 1] * (1.0 / pivot[:, at : at + 1])
        work = work - jnp.where(down > step, ratio, 0.0) * pivot
    pivots = jnp.sum(jnp.where(diagonal, work[:, eig_count:], 0.0), axis=1, keepdims=True)
    inverse = work[:, :eig_count] * lax.rsqrt(pivots)
    out_ref[...] = jnp.dot(
        inverse, smoothed, precision=lax.Precision.HIGHEST, preferred_element_type=jnp.float32
    )

    for item in FIRST_SENDS + sum(RELAYS.values(), ()):
        for copy in unit_copies(*item):
            copy.wait_send()
    for step in range(1, col_count):
        part_copy(step).wait_send()


def per_device_full(total_rows, row_count, embeddings, vectors, block_pairs):
    del block_pairs
    eig_count, block_rows = vectors.shape
    near_rows, width = embeddings.shape
    col_count = near_rows // block_rows
    half = block_rows // 2
    padded = eig_count + 8
    dma = pltpu.SemaphoreType.DMA
    return pl.pallas_call(
        functools.partial(whole_kernel, total_rows),
        out_shape=jax.ShapeDtypeStruct((eig_count, block_rows), jnp.float32),
        in_specs=[pl.BlockSpec(memory_space=pl.ANY), pl.BlockSpec(memory_space=pltpu.VMEM)],
        out_specs=pl.BlockSpec(memory_space=pltpu.VMEM),
        scratch_shapes=[
            pltpu.VMEM((near_rows, width), jnp.bfloat16),
            pltpu.VMEM((UNITS, half, width), jnp.bfloat16),
            pltpu.VMEM((UNITS, eig_count, half), jnp.bfloat16),
            pltpu.VMEM((col_count, 8, block_rows), jnp.float32),
            pltpu.VMEM((col_count, padded, block_rows), jnp.float32),
            pltpu.VMEM((col_count - 1, padded, block_rows), jnp.float32),
            pltpu.VMEM((row_count, eig_count, eig_count), jnp.float32),
            pltpu.VMEM((col_count, eig_count, eig_count), jnp.float32),
            dma(()),
            dma((UNITS,)),
            dma((UNITS,)),
            dma((UNITS,)),
            dma((UNITS,)),
            dma((col_count - 1,)),
            dma((col_count - 1,)),
            dma((row_count - 1,)),
            dma((row_count - 1,)),
            dma((col_count - 1,)),
            dma((col_count - 1,)),
        ],
        compiler_params=pltpu.CompilerParams(
            collective_id=0, has_side_effects=True, vmem_limit_bytes=48 * 1024 * 1024
        ),
    )(embeddings, vectors)


def solution(mesh):
    row_count, col_count = mesh.shape["row"], mesh.shape["col"]

    def step(embeddings, vectors, block_pairs):
        blocks = row_count * col_count
        full = block_pairs.shape[0] == blocks * (blocks - 1) and row_count == 8
        body = per_device
        if full:
            body = functools.partial(per_device_full, embeddings.shape[0], row_count)
        return jax.shard_map(
            body,
            mesh=mesh,
            in_specs=(P("row", None), P(None, ("row", "col")), P()),
            out_specs=P(None, ("row", "col")),
            check_vma=False,
        )(embeddings, vectors, block_pairs)

    return step
```

```python
import functools
import math

import jax
import jax.numpy as jnp
from jax import lax
from jax.experimental import pallas as pl
from jax.experimental.pallas import tpu as pltpu
from jax.sharding import PartitionSpec as P


def inverse_norms(blocks):
    return lax.rsqrt(jnp.mean(jnp.square(blocks.astype(jnp.float32)), axis=-1) + 1e-06)


def tile_terms(rows_x, cols_x, norm_rows, norm_cols, cols_v, feature_width):
    scores = jnp.dot(rows_x, cols_x.T, preferred_element_type=jnp.float32)
    affinity = jnp.exp(scores * norm_rows[:, None] * norm_cols[None, :] / math.sqrt(feature_width))
    rounded = affinity.astype(jnp.bfloat16)
    contrib = jnp.dot(cols_v, rounded.T, preferred_element_type=jnp.float32)
    return (contrib, jnp.sum(affinity, axis=1))


def tile_mask(block_pairs, near_column, col_count, row_count, here_row, here_col):
    near_ids = block_pairs[:, near_column]
    far_ids = block_pairs[:, 1 - near_column]
    member = (near_ids // col_count == here_row) & (far_ids % col_count == here_col)
    near_hot = ((near_ids % col_count)[:, None] == jnp.arange(col_count)[None, :]) & member[:, None]
    far_hot = (far_ids // col_count)[:, None] == jnp.arange(row_count)[None, :]
    return jnp.dot(
        near_hot.astype(jnp.float32).T,
        far_hot.astype(jnp.float32),
        preferred_element_type=jnp.float32,
    )


def add_block(running, contrib, row_totals, column_start, block_rows):
    sums_now, degree_now = running
    old_sums = lax.dynamic_slice_in_dim(sums_now, column_start, block_rows, 1)
    sums_now = lax.dynamic_update_slice_in_dim(sums_now, old_sums + contrib, column_start, 1)
    old_degree = lax.dynamic_slice_in_dim(degree_now, column_start, block_rows, 1)
    degree_now = lax.dynamic_update_slice_in_dim(
        degree_now, old_degree + row_totals[None, :], column_start, 1
    )
    return (sums_now, degree_now)


def per_device(embeddings, vectors, block_pairs):
    col_count = lax.axis_size("col")
    row_count = lax.axis_size("row")
    here_row = lax.axis_index("row")
    here_col = lax.axis_index("col")
    eig_count, block_rows = vectors.shape
    feature_width = embeddings.shape[1]
    near_blocks = embeddings.reshape(col_count, block_rows, feature_width)
    near_norms = inverse_norms(near_blocks)
    own_block = lax.dynamic_slice_in_dim(near_blocks, here_col, 1, 0)
    present = tile_mask(block_pairs, 0, col_count, row_count, here_row, here_col)
    start_sums = jnp.zeros((eig_count, col_count * block_rows), jnp.float32)
    start_degree = jnp.zeros((1, col_count * block_rows), jnp.float32)
    far_x = lax.all_gather(own_block, "row", axis=0, tiled=True)
    far_v = lax.all_gather(vectors[None], "row", axis=0, tiled=True)
    far_norms = inverse_norms(far_x)
    piece_blocks = far_x.shape[0]

    def visit(position, current):
        far_index = position // col_count
        near_index = position % col_count

        def compute(totals):
            contrib, row_totals = tile_terms(
                near_blocks[near_index],
                far_x[far_index],
                near_norms[near_index],
                far_norms[far_index],
                far_v[far_index],
                feature_width,
            )
            return add_block(totals, contrib, row_totals, near_index * block_rows, block_rows)

        return lax.cond(
            present[near_index, far_index] > 0.5, compute, lambda totals: totals, current
        )

    partial_sums, degree = lax.fori_loop(
        0, piece_blocks * col_count, visit, (start_sums, start_degree)
    )
    owned_sums, owned_degree = (
        lax.psum_scatter(partial_sums, "col", scatter_dimension=1, tiled=True),
        lax.psum_scatter(degree, "col", scatter_dimension=1, tiled=True),
    )
    smoothed = owned_sums / owned_degree
    total_rows = block_rows * col_count * row_count
    local_gram = jnp.dot(
        smoothed, smoothed.T, precision=lax.Precision.HIGHEST, preferred_element_type=jnp.float32
    )
    gram_matrix = lax.psum(local_gram, ("row", "col")) / total_rows
    factor = jnp.linalg.cholesky(gram_matrix)
    return lax.linalg.triangular_solve(factor, smoothed, left_side=True, lower=True)


UNITS = 16
FIRST_SENDS = ((0, 4, 2), (1, 5, 4), (0, 2, 1), (1, 3, 1), (1, 8, 2), (0, 9, 4))
RELAYS = {
    4: ((4, 12, 4), (5, 13, 2), (4, 6, 1), (5, 7, 1)),
    8: ((8, 10, 1), (9, 11, 1)),
    12: ((12, 14, 1), (13, 15, 1)),
}


def across(row, bits):
    if bits & 1:
        row = row + 1 - 2 * (row % 2)
    if bits & 2:
        row = row + 2 - 4 * ((row // 2) % 2)
    if bits & 4:
        row = row + 4 - 8 * ((row // 4) % 2)
    return row


def whole_kernel(
    total_rows,
    x_hbm,
    v_hbm,
    out_ref,
    own_x,
    turned_x,
    own_v,
    far_x,
    far_v,
    own_norm,
    acc,
    parts,
    plane_gram,
    depth_gram,
    own_sem,
    own_v_sem,
    x_send,
    x_recv,
    v_send,
    v_recv,
    part_send,
    part_recv,
    plane_send,
    plane_recv,
    depth_send,
    depth_recv,
):
    row = lax.axis_index("row")
    col = lax.axis_index("col")
    row_count = plane_gram.shape[0]
    col_count, padded, block_rows = acc.shape
    eig_count = own_v.shape[0]
    half = block_rows // 2
    width = own_x.shape[1]
    mesh_ids = pl.DeviceIdType.MESH

    load = pltpu.make_async_copy(x_hbm, own_x, own_sem)
    load.start()
    load_v = pltpu.make_async_copy(v_hbm, own_v, own_v_sem)
    load_v.start()

    barrier = pltpu.get_barrier_semaphore()
    for bits in range(1, row_count):
        pl.semaphore_signal(barrier, inc=1, device_id=(across(row, bits), col), device_id_type=mesh_ids)
    for step in range(1, col_count):
        pl.semaphore_signal(barrier, inc=1, device_id=(row, (col + step) % col_count), device_id_type=mesh_ids)
    pl.semaphore_wait(barrier, row_count + col_count - 2)

    def unit_copies(source, target, bits):
        if source < 2:
            start = pl.multiple_of(col * block_rows + source * half, half)
            x_src = x_hbm.at[pl.ds(start, half), :]
            v_src = v_hbm.at[:, pl.ds(source * half, half)]
        else:
            x_src = far_x.at[source]
            v_src = far_v.at[source]
        partner = (across(row, bits), col)
        return (
            pltpu.make_async_remote_copy(
                src_ref=v_src, dst_ref=far_v.at[target], send_sem=v_send.at[target],
                recv_sem=v_recv.at[target], device_id=partner, device_id_type=mesh_ids,
            ),
            pltpu.make_async_remote_copy(
                src_ref=x_src, dst_ref=far_x.at[target], send_sem=x_send.at[target],
                recv_sem=x_recv.at[target], device_id=partner, device_id_type=mesh_ids,
            ),
        )

    def start_unit(item):
        for copy in unit_copies(*item):
            copy.start()

    def wait_unit(target):
        pltpu.make_async_copy(far_v.at[target], far_v.at[target], v_recv.at[target]).wait()
        pltpu.make_async_copy(far_x.at[target], far_x.at[target], x_recv.at[target]).wait()

    for item in FIRST_SENDS:
        start_unit(item)

    load.wait()
    load_v.wait()
    far_v[0] = own_v[:, :half]
    far_v[1] = own_v[:, half:]
    for part in range(2):
        start = pl.multiple_of(col * block_rows + part * half, half)
        far_x[part] = own_x[pl.ds(start, half), :]
    acc[...] = jnp.zeros_like(acc)

    @pl.loop(0, col_count)
    def _(near):
        rows = own_x[pl.ds(pl.multiple_of(near * block_rows, block_rows), block_rows), :]
        turned = rows.astype(jnp.float32).T
        turned_x[near] = turned.astype(jnp.bfloat16)
        mean = jnp.sum(turned * turned, axis=0, keepdims=True) * (1.0 / width)
        own_norm[near] = jnp.broadcast_to(lax.rsqrt(mean + 1e-06), (8, block_rows))

    scale = 1.4426950408889634 / math.sqrt(width)

    @pl.loop(0, UNITS)
    def _(unit):
        @pl.when(unit == 2)
        def _():
            acc[col] = jnp.zeros((padded, block_rows), jnp.float32)

        for first, items in RELAYS.items():
            @pl.when(unit == first)
            def _(first=first, items=items):
                wait_unit(first)
                wait_unit(first + 1)
                for item in items:
                    start_unit(item)

        for alone in (2, 3, 6, 7, 10, 11, 14, 15):
            @pl.when(unit == alone)
            def _(alone=alone):
                wait_unit(alone)

        cols = far_x[unit]
        wide = cols.astype(jnp.float32)
        mean = jnp.sum(wide * wide, axis=1, keepdims=True) * (1.0 / width)
        col_norm = lax.rsqrt(mean + 1e-06) * scale
        cols_v = far_v[unit]
        for near in range(col_count):
            scores = jnp.dot(cols, turned_x[near], preferred_element_type=jnp.float32)
            affinity = jnp.exp2(scores * own_norm[near, 0:1, :] * col_norm)
            acc[near, eig_count:, :] += jnp.sum(affinity.reshape(half // 8, 8, block_rows), axis=0)
            acc[near, :eig_count, :] += jnp.dot(
                cols_v, affinity.astype(jnp.bfloat16), preferred_element_type=jnp.float32
            )

    def part_copy(step):
        target = (col + step) % col_count
        return pltpu.make_async_remote_copy(
            src_ref=acc.at[target], dst_ref=parts.at[step - 1], send_sem=part_send.at[step - 1],
            recv_sem=part_recv.at[step - 1], device_id=(row, target), device_id_type=mesh_ids,
        )

    for step in range(1, col_count):
        part_copy(step).start()
    total = acc[col]
    for step in range(1, col_count):
        part_copy(step).wait_recv()
        total = total + parts[step - 1]
    degree = jnp.sum(total[eig_count:, :], axis=0, keepdims=True)
    smoothed = total[:eig_count, :] / degree

    def gram_sum(gram, held, me, partners, send_sem, recv_sem):
        held[me] = gram
        copies = []
        for at, partner in enumerate(partners):
            copies.append(
                pltpu.make_async_remote_copy(
                    src_ref=held.at[me], dst_ref=held.at[me], send_sem=send_sem.at[at],
                    recv_sem=recv_sem.at[at], device_id=partner, device_id_type=mesh_ids,
                )
            )
        for copy in copies:
            copy.start()
        for copy in copies:
            copy.wait()
        return jnp.sum(held[...], axis=0)

    gram = lax.dot_general(
        smoothed, smoothed, (((1,), (1,)), ((), ())),
        precision=lax.Precision.HIGHEST, preferred_element_type=jnp.float32,
    )
    gram = gram_sum(
        gram, plane_gram, row, [(across(row, bits), col) for bits in range(1, row_count)],
        plane_send, plane_recv,
    )
    gram = gram_sum(
        gram, depth_gram, col, [(row, (col + step) % col_count) for step in range(1, col_count)],
        depth_send, depth_recv,
    )
    gram = gram / total_rows

    down = lax.broadcasted_iota(jnp.int32, (eig_count, 1), 0)
    at_row = lax.broadcasted_iota(jnp.int32, (eig_count, eig_count), 0)
    at_col = lax.broadcasted_iota(jnp.int32, (eig_count, eig_count), 1)
    diagonal = at_row == at_col
    work = jnp.concatenate([diagonal.astype(jnp.float32), gram], axis=1)
    for step in range(eig_count - 1):
        at = eig_count + step
        pivot = work[step : step + 1, :]
        ratio = work[:, at : at + 1] * (1.0 / pivot[:, at : at + 1])
        work = work - jnp.where(down > step, ratio, 0.0) * pivot
    pivots = jnp.sum(jnp.where(diagonal, work[:, eig_count:], 0.0), axis=1, keepdims=True)
    inverse = work[:, :eig_count] * lax.rsqrt(pivots)
    out_ref[...] = jnp.dot(
        inverse, smoothed, precision=lax.Precision.HIGHEST, preferred_element_type=jnp.float32
    )

    for item in FIRST_SENDS + sum(RELAYS.values(), ()):
        for copy in unit_copies(*item):
            copy.wait_send()
    for step in range(1, col_count):
        part_copy(step).wait_send()


def per_device_full(total_rows, row_count, embeddings, vectors, block_pairs):
    del block_pairs
    eig_count, block_rows = vectors.shape
    near_rows, width = embeddings.shape
    col_count = near_rows // block_rows
    half = block_rows // 2
    padded = eig_count + 8
    dma = pltpu.SemaphoreType.DMA
    return pl.pallas_call(
        functools.partial(whole_kernel, total_rows),
        out_shape=jax.ShapeDtypeStruct((eig_count, block_rows), jnp.float32),
        in_specs=[pl.BlockSpec(memory_space=pl.ANY)] * 2,
        out_specs=pl.BlockSpec(memory_space=pltpu.VMEM),
        scratch_shapes=[
            pltpu.VMEM((near_rows, width), jnp.bfloat16),
            pltpu.VMEM((col_count, width, block_rows), jnp.bfloat16),
            pltpu.VMEM((eig_count, block_rows), jnp.bfloat16),
            pltpu.VMEM((UNITS, half, width), jnp.bfloat16),
            pltpu.VMEM((UNITS, eig_count, half), jnp.bfloat16),
            pltpu.VMEM((col_count, 8, block_rows), jnp.float32),
            pltpu.VMEM((col_count, padded, block_rows), jnp.float32),
            pltpu.VMEM((col_count - 1, padded, block_rows), jnp.float32),
            pltpu.VMEM((row_count, eig_count, eig_count), jnp.float32),
            pltpu.VMEM((col_count, eig_count, eig_count), jnp.float32),
            dma(()),
            dma(()),
            dma((UNITS,)),
            dma((UNITS,)),
            dma((UNITS,)),
            dma((UNITS,)),
            dma((col_count - 1,)),
            dma((col_count - 1,)),
            dma((row_count - 1,)),
            dma((row_count - 1,)),
            dma((col_count - 1,)),
            dma((col_count - 1,)),
        ],
        compiler_params=pltpu.CompilerParams(
            collective_id=0, has_side_effects=True, vmem_limit_bytes=60 * 1024 * 1024
        ),
    )(embeddings, vectors)


def solution(mesh):
    row_count, col_count = mesh.shape["row"], mesh.shape["col"]

    def step(embeddings, vectors, block_pairs):
        blocks = row_count * col_count
        full = block_pairs.shape[0] == blocks * (blocks - 1) and row_count == 8
        body = per_device
        if full:
            body = functools.partial(per_device_full, embeddings.shape[0], row_count)
        return jax.shard_map(
            body,
            mesh=mesh,
            in_specs=(P("row", None), P(None, ("row", "col")), P()),
            out_specs=P(None, ("row", "col")),
            check_vma=False,
        )(embeddings, vectors, block_pairs)

    return step
```

```python
import functools
import math

import jax
import jax.numpy as jnp
from jax import lax
from jax.experimental import pallas as pl
from jax.experimental.pallas import tpu as pltpu
from jax.sharding import PartitionSpec as P


def inverse_norms(blocks):
    return lax.rsqrt(jnp.mean(jnp.square(blocks.astype(jnp.float32)), axis=-1) + 1e-06)


def tile_terms(rows_x, cols_x, norm_rows, norm_cols, cols_v, feature_width):
    scores = jnp.dot(rows_x, cols_x.T, preferred_element_type=jnp.float32)
    affinity = jnp.exp(scores * norm_rows[:, None] * norm_cols[None, :] / math.sqrt(feature_width))
    rounded = affinity.astype(jnp.bfloat16)
    contrib = jnp.dot(cols_v, rounded.T, preferred_element_type=jnp.float32)
    return (contrib, jnp.sum(affinity, axis=1))


def tile_mask(block_pairs, near_column, col_count, row_count, here_row, here_col):
    near_ids = block_pairs[:, near_column]
    far_ids = block_pairs[:, 1 - near_column]
    member = (near_ids // col_count == here_row) & (far_ids % col_count == here_col)
    near_hot = ((near_ids % col_count)[:, None] == jnp.arange(col_count)[None, :]) & member[:, None]
    far_hot = (far_ids // col_count)[:, None] == jnp.arange(row_count)[None, :]
    return jnp.dot(
        near_hot.astype(jnp.float32).T,
        far_hot.astype(jnp.float32),
        preferred_element_type=jnp.float32,
    )


def add_block(running, contrib, row_totals, column_start, block_rows):
    sums_now, degree_now = running
    old_sums = lax.dynamic_slice_in_dim(sums_now, column_start, block_rows, 1)
    sums_now = lax.dynamic_update_slice_in_dim(sums_now, old_sums + contrib, column_start, 1)
    old_degree = lax.dynamic_slice_in_dim(degree_now, column_start, block_rows, 1)
    degree_now = lax.dynamic_update_slice_in_dim(
        degree_now, old_degree + row_totals[None, :], column_start, 1
    )
    return (sums_now, degree_now)


def per_device(embeddings, vectors, block_pairs):
    col_count = lax.axis_size("col")
    row_count = lax.axis_size("row")
    here_row = lax.axis_index("row")
    here_col = lax.axis_index("col")
    eig_count, block_rows = vectors.shape
    feature_width = embeddings.shape[1]
    near_blocks = embeddings.reshape(col_count, block_rows, feature_width)
    near_norms = inverse_norms(near_blocks)
    own_block = lax.dynamic_slice_in_dim(near_blocks, here_col, 1, 0)
    present = tile_mask(block_pairs, 0, col_count, row_count, here_row, here_col)
    start_sums = jnp.zeros((eig_count, col_count * block_rows), jnp.float32)
    start_degree = jnp.zeros((1, col_count * block_rows), jnp.float32)
    far_x = lax.all_gather(own_block, "row", axis=0, tiled=True)
    far_v = lax.all_gather(vectors[None], "row", axis=0, tiled=True)
    far_norms = inverse_norms(far_x)
    piece_blocks = far_x.shape[0]

    def visit(position, current):
        far_index = position // col_count
        near_index = position % col_count

        def compute(totals):
            contrib, row_totals = tile_terms(
                near_blocks[near_index],
                far_x[far_index],
                near_norms[near_index],
                far_norms[far_index],
                far_v[far_index],
                feature_width,
            )
            return add_block(totals, contrib, row_totals, near_index * block_rows, block_rows)

        return lax.cond(
            present[near_index, far_index] > 0.5, compute, lambda totals: totals, current
        )

    partial_sums, degree = lax.fori_loop(
        0, piece_blocks * col_count, visit, (start_sums, start_degree)
    )
    owned_sums, owned_degree = (
        lax.psum_scatter(partial_sums, "col", scatter_dimension=1, tiled=True),
        lax.psum_scatter(degree, "col", scatter_dimension=1, tiled=True),
    )
    smoothed = owned_sums / owned_degree
    total_rows = block_rows * col_count * row_count
    local_gram = jnp.dot(
        smoothed, smoothed.T, precision=lax.Precision.HIGHEST, preferred_element_type=jnp.float32
    )
    gram_matrix = lax.psum(local_gram, ("row", "col")) / total_rows
    factor = jnp.linalg.cholesky(gram_matrix)
    return lax.linalg.triangular_solve(factor, smoothed, left_side=True, lower=True)


UNITS = 16
FIRST_SENDS = ((0, 4, 2), (1, 5, 4), (0, 2, 1), (1, 3, 1), (1, 8, 2), (0, 9, 4))
RELAYS = {
    4: ((4, 12, 4), (5, 13, 2), (4, 6, 1), (5, 7, 1)),
    8: ((8, 10, 1), (9, 11, 1)),
    12: ((12, 14, 1), (13, 15, 1)),
}


def across(row, bits):
    if bits & 1:
        row = row + 1 - 2 * (row % 2)
    if bits & 2:
        row = row + 2 - 4 * ((row // 2) % 2)
    if bits & 4:
        row = row + 4 - 8 * ((row // 4) % 2)
    return row


def whole_kernel(
    total_rows,
    x_hbm,
    v_hbm,
    out_ref,
    own_x,
    turned_x,
    own_v,
    far_x,
    far_v,
    own_norm,
    acc,
    parts,
    plane_gram,
    depth_gram,
    own_sem,
    own_v_sem,
    x_send,
    x_recv,
    v_send,
    v_recv,
    part_send,
    part_recv,
    plane_send,
    plane_recv,
    depth_send,
    depth_recv,
):
    row = lax.axis_index("row")
    col = lax.axis_index("col")
    row_count = plane_gram.shape[0]
    col_count, padded, block_rows = acc.shape
    eig_count = own_v.shape[0]
    half = block_rows // 2
    width = own_x.shape[1]
    mesh_ids = pl.DeviceIdType.MESH

    load = pltpu.make_async_copy(x_hbm, own_x, own_sem)
    load.start()
    load_v = pltpu.make_async_copy(v_hbm, own_v, own_v_sem)
    load_v.start()

    barrier = pltpu.get_barrier_semaphore()
    for bits in range(1, row_count):
        pl.semaphore_signal(barrier, inc=1, device_id=(across(row, bits), col), device_id_type=mesh_ids)
    for step in range(1, col_count):
        pl.semaphore_signal(barrier, inc=1, device_id=(row, (col + step) % col_count), device_id_type=mesh_ids)
    pl.semaphore_wait(barrier, row_count + col_count - 2)

    def unit_copies(source, target, bits):
        if source < 2:
            start = pl.multiple_of(col * block_rows + source * half, half)
            x_src = x_hbm.at[pl.ds(start, half), :]
            v_src = v_hbm.at[:, pl.ds(source * half, half)]
        else:
            x_src = far_x.at[source]
            v_src = far_v.at[source]
        partner = (across(row, bits), col)
        return (
            pltpu.make_async_remote_copy(
                src_ref=v_src, dst_ref=far_v.at[target], send_sem=v_send.at[target],
                recv_sem=v_recv.at[target], device_id=partner, device_id_type=mesh_ids,
            ),
            pltpu.make_async_remote_copy(
                src_ref=x_src, dst_ref=far_x.at[target], send_sem=x_send.at[target],
                recv_sem=x_recv.at[target], device_id=partner, device_id_type=mesh_ids,
            ),
        )

    def start_unit(item):
        for copy in unit_copies(*item):
            copy.start()

    def wait_unit(target):
        pltpu.make_async_copy(far_v.at[target], far_v.at[target], v_recv.at[target]).wait()
        pltpu.make_async_copy(far_x.at[target], far_x.at[target], x_recv.at[target]).wait()

    for item in FIRST_SENDS:
        start_unit(item)

    load.wait()
    load_v.wait()
    far_v[0] = own_v[:, :half]
    far_v[1] = own_v[:, half:]
    for part in range(2):
        start = pl.multiple_of(col * block_rows + part * half, half)
        far_x[part] = own_x[pl.ds(start, half), :]
    acc[...] = jnp.zeros_like(acc)

    @pl.loop(0, col_count)
    def _(near):
        rows = own_x[pl.ds(pl.multiple_of(near * block_rows, block_rows), block_rows), :]
        turned = rows.astype(jnp.float32).T
        turned_x[near] = turned.astype(jnp.bfloat16)
        mean = jnp.sum(turned * turned, axis=0, keepdims=True) * (1.0 / width)
        own_norm[near] = jnp.broadcast_to(lax.rsqrt(mean + 1e-06), (8, block_rows))

    scale = 1.4426950408889634 / math.sqrt(width)

    def unit_norm(unit):
        wide = far_x[unit].astype(jnp.float32)
        mean = jnp.sum(wide * wide, axis=1, keepdims=True) * (1.0 / width)
        return lax.rsqrt(mean + 1e-06) * scale

    def add_tile(unit, near, col_norm):
        scores = jnp.dot(far_x[unit], turned_x[near], preferred_element_type=jnp.float32)
        affinity = jnp.exp2(scores * own_norm[near, 0:1, :] * col_norm)
        acc[near, eig_count:, :] += jnp.sum(affinity.reshape(half // 8, 8, block_rows), axis=0)
        acc[near, :eig_count, :] += jnp.dot(
            far_v[unit], affinity.astype(jnp.bfloat16), preferred_element_type=jnp.float32
        )

    @pl.loop(0, UNITS - 2)
    def _(unit):
        @pl.when(unit == 2)
        def _():
            acc[col] = jnp.zeros((padded, block_rows), jnp.float32)

        for first, items in RELAYS.items():
            @pl.when(unit == first)
            def _(first=first, items=items):
                wait_unit(first)
                wait_unit(first + 1)
                for item in items:
                    start_unit(item)

        for alone in (2, 3, 6, 7, 10, 11):
            @pl.when(unit == alone)
            def _(alone=alone):
                wait_unit(alone)

        col_norm = unit_norm(unit)
        for near in range(col_count):
            add_tile(unit, near, col_norm)

    pair = col + 1 - 2 * (col % 2)
    far = (col + 2) % col_count
    far_pair = col_count - 1 - col

    def part_copy(at):
        source, target = ((far_pair, pair), (pair, pair), (far, far))[at]
        return pltpu.make_async_remote_copy(
            src_ref=acc.at[source], dst_ref=parts.at[at], send_sem=part_send.at[at],
            recv_sem=part_recv.at[at], device_id=(row, target), device_id_type=mesh_ids,
        )

    last = (UNITS - 2, UNITS - 1)
    for unit in last:
        wait_unit(unit)
    last_norms = [unit_norm(unit) for unit in last]
    for at, near in enumerate((far_pair, pair, far, col)):
        for unit, col_norm in zip(last, last_norms):
            add_tile(unit, near, col_norm)
        if at == 2:
            part_copy(0).wait_recv()
            acc[far] = acc[far] + parts[0]
        if at < 3:
            part_copy(at).start()
    part_copy(1).wait_recv()
    part_copy(2).wait_recv()
    total = acc[col] + parts[1] + parts[2]
    degree = jnp.sum(total[eig_count:, :], axis=0, keepdims=True)
    smoothed = total[:eig_count, :] / degree

    def gram_sum(gram, held, me, partners, send_sem, recv_sem):
        held[me] = gram
        copies = []
        for at, partner in enumerate(partners):
            copies.append(
                pltpu.make_async_remote_copy(
                    src_ref=held.at[me], dst_ref=held.at[me], send_sem=send_sem.at[at],
                    recv_sem=recv_sem.at[at], device_id=partner, device_id_type=mesh_ids,
                )
            )
        for copy in copies:
            copy.start()
        for copy in copies:
            copy.wait()
        return jnp.sum(held[...], axis=0)

    gram = lax.dot_general(
        smoothed, smoothed, (((1,), (1,)), ((), ())),
        precision=lax.Precision.HIGHEST, preferred_element_type=jnp.float32,
    )
    packed = jnp.concatenate([gram[: eig_count // 2, :], gram[eig_count // 2 :, :]], axis=1)
    packed = gram_sum(
        packed, plane_gram, row, [(across(row, bits), col) for bits in range(1, row_count)],
        plane_send, plane_recv,
    )
    packed = gram_sum(
        packed, depth_gram, col, [(row, (col + step) % col_count) for step in range(1, col_count)],
        depth_send, depth_recv,
    )
    gram = jnp.concatenate([packed[:, :eig_count], packed[:, eig_count:]], axis=0) / total_rows

    down = lax.broadcasted_iota(jnp.int32, (eig_count, 1), 0)
    at_row = lax.broadcasted_iota(jnp.int32, (eig_count, eig_count), 0)
    at_col = lax.broadcasted_iota(jnp.int32, (eig_count, eig_count), 1)
    diagonal = at_row == at_col
    work = jnp.concatenate([diagonal.astype(jnp.float32), gram], axis=1)
    for step in range(eig_count - 1):
        at = eig_count + step
        pivot = work[step : step + 1, :]
        ratio = work[:, at : at + 1] * (1.0 / pivot[:, at : at + 1])
        work = work - jnp.where(down > step, ratio, 0.0) * pivot
    pivots = jnp.sum(jnp.where(diagonal, work[:, eig_count:], 0.0), axis=1, keepdims=True)
    inverse = work[:, :eig_count] * lax.rsqrt(pivots)
    out_ref[...] = jnp.dot(
        inverse, smoothed, precision=lax.Precision.HIGHEST, preferred_element_type=jnp.float32
    )

    for item in FIRST_SENDS + sum(RELAYS.values(), ()):
        for copy in unit_copies(*item):
            copy.wait_send()
    for at in range(3):
        part_copy(at).wait_send()


def per_device_full(total_rows, row_count, embeddings, vectors, block_pairs):
    del block_pairs
    eig_count, block_rows = vectors.shape
    near_rows, width = embeddings.shape
    col_count = near_rows // block_rows
    half = block_rows // 2
    padded = eig_count + 8
    dma = pltpu.SemaphoreType.DMA
    return pl.pallas_call(
        functools.partial(whole_kernel, total_rows),
        out_shape=jax.ShapeDtypeStruct((eig_count, block_rows), jnp.float32),
        in_specs=[pl.BlockSpec(memory_space=pl.ANY)] * 2,
        out_specs=pl.BlockSpec(memory_space=pltpu.VMEM),
        scratch_shapes=[
            pltpu.VMEM((near_rows, width), jnp.bfloat16),
            pltpu.VMEM((col_count, width, block_rows), jnp.bfloat16),
            pltpu.VMEM((eig_count, block_rows), jnp.bfloat16),
            pltpu.VMEM((UNITS, half, width), jnp.bfloat16),
            pltpu.VMEM((UNITS, eig_count, half), jnp.bfloat16),
            pltpu.VMEM((col_count, 8, block_rows), jnp.float32),
            pltpu.VMEM((col_count, padded, block_rows), jnp.float32),
            pltpu.VMEM((col_count - 1, padded, block_rows), jnp.float32),
            pltpu.VMEM((row_count, eig_count // 2, 2 * eig_count), jnp.float32),
            pltpu.VMEM((col_count, eig_count // 2, 2 * eig_count), jnp.float32),
            dma(()),
            dma(()),
            dma((UNITS,)),
            dma((UNITS,)),
            dma((UNITS,)),
            dma((UNITS,)),
            dma((col_count - 1,)),
            dma((col_count - 1,)),
            dma((row_count - 1,)),
            dma((row_count - 1,)),
            dma((col_count - 1,)),
            dma((col_count - 1,)),
        ],
        compiler_params=pltpu.CompilerParams(
            collective_id=0, has_side_effects=True, vmem_limit_bytes=60 * 1024 * 1024
        ),
    )(embeddings, vectors)


def solution(mesh):
    row_count, col_count = mesh.shape["row"], mesh.shape["col"]

    def step(embeddings, vectors, block_pairs):
        blocks = row_count * col_count
        full = block_pairs.shape[0] == blocks * (blocks - 1) and (row_count, col_count) == (8, 4)
        body = per_device
        if full:
            body = functools.partial(per_device_full, embeddings.shape[0], row_count)
        return jax.shard_map(
            body,
            mesh=mesh,
            in_specs=(P("row", None), P(None, ("row", "col")), P()),
            out_specs=P(None, ("row", "col")),
            check_vma=False,
        )(embeddings, vectors, block_pairs)

    return step
```

```python
import functools
import math

import jax
import jax.numpy as jnp
from jax import lax
from jax.experimental import pallas as pl
from jax.experimental.pallas import tpu as pltpu
from jax.sharding import PartitionSpec as P


def inverse_norms(blocks):
    return lax.rsqrt(jnp.mean(jnp.square(blocks.astype(jnp.float32)), axis=-1) + 1e-06)


def tile_terms(rows_x, cols_x, norm_rows, norm_cols, cols_v, feature_width):
    scores = jnp.dot(rows_x, cols_x.T, preferred_element_type=jnp.float32)
    affinity = jnp.exp(scores * norm_rows[:, None] * norm_cols[None, :] / math.sqrt(feature_width))
    rounded = affinity.astype(jnp.bfloat16)
    contrib = jnp.dot(cols_v, rounded.T, preferred_element_type=jnp.float32)
    return (contrib, jnp.sum(affinity, axis=1))


def tile_mask(block_pairs, near_column, col_count, row_count, here_row, here_col):
    near_ids = block_pairs[:, near_column]
    far_ids = block_pairs[:, 1 - near_column]
    member = (near_ids // col_count == here_row) & (far_ids % col_count == here_col)
    near_hot = ((near_ids % col_count)[:, None] == jnp.arange(col_count)[None, :]) & member[:, None]
    far_hot = (far_ids // col_count)[:, None] == jnp.arange(row_count)[None, :]
    return jnp.dot(
        near_hot.astype(jnp.float32).T,
        far_hot.astype(jnp.float32),
        preferred_element_type=jnp.float32,
    )


def add_block(running, contrib, row_totals, column_start, block_rows):
    sums_now, degree_now = running
    old_sums = lax.dynamic_slice_in_dim(sums_now, column_start, block_rows, 1)
    sums_now = lax.dynamic_update_slice_in_dim(sums_now, old_sums + contrib, column_start, 1)
    old_degree = lax.dynamic_slice_in_dim(degree_now, column_start, block_rows, 1)
    degree_now = lax.dynamic_update_slice_in_dim(
        degree_now, old_degree + row_totals[None, :], column_start, 1
    )
    return (sums_now, degree_now)


def per_device(embeddings, vectors, block_pairs):
    col_count = lax.axis_size("col")
    row_count = lax.axis_size("row")
    here_row = lax.axis_index("row")
    here_col = lax.axis_index("col")
    eig_count, block_rows = vectors.shape
    feature_width = embeddings.shape[1]
    near_blocks = embeddings.reshape(col_count, block_rows, feature_width)
    near_norms = inverse_norms(near_blocks)
    own_block = lax.dynamic_slice_in_dim(near_blocks, here_col, 1, 0)
    present = tile_mask(block_pairs, 0, col_count, row_count, here_row, here_col)
    start_sums = jnp.zeros((eig_count, col_count * block_rows), jnp.float32)
    start_degree = jnp.zeros((1, col_count * block_rows), jnp.float32)
    far_x = lax.all_gather(own_block, "row", axis=0, tiled=True)
    far_v = lax.all_gather(vectors[None], "row", axis=0, tiled=True)
    far_norms = inverse_norms(far_x)
    piece_blocks = far_x.shape[0]

    def visit(position, current):
        far_index = position // col_count
        near_index = position % col_count

        def compute(totals):
            contrib, row_totals = tile_terms(
                near_blocks[near_index],
                far_x[far_index],
                near_norms[near_index],
                far_norms[far_index],
                far_v[far_index],
                feature_width,
            )
            return add_block(totals, contrib, row_totals, near_index * block_rows, block_rows)

        return lax.cond(
            present[near_index, far_index] > 0.5, compute, lambda totals: totals, current
        )

    partial_sums, degree = lax.fori_loop(
        0, piece_blocks * col_count, visit, (start_sums, start_degree)
    )
    owned_sums, owned_degree = (
        lax.psum_scatter(partial_sums, "col", scatter_dimension=1, tiled=True),
        lax.psum_scatter(degree, "col", scatter_dimension=1, tiled=True),
    )
    smoothed = owned_sums / owned_degree
    total_rows = block_rows * col_count * row_count
    local_gram = jnp.dot(
        smoothed, smoothed.T, precision=lax.Precision.HIGHEST, preferred_element_type=jnp.float32
    )
    gram_matrix = lax.psum(local_gram, ("row", "col")) / total_rows
    factor = jnp.linalg.cholesky(gram_matrix)
    return lax.linalg.triangular_solve(factor, smoothed, left_side=True, lower=True)


UNITS = 16
FIRST_SENDS = ((0, 4, 2), (1, 5, 4), (0, 2, 1), (1, 3, 1), (1, 8, 2), (0, 9, 4))
RELAYS = {
    4: ((4, 12, 4), (5, 13, 2), (4, 6, 1), (5, 7, 1)),
    8: ((8, 10, 1), (9, 11, 1)),
    12: ((12, 14, 1), (13, 15, 1)),
}


def across(row, bits):
    if bits & 1:
        row = row + 1 - 2 * (row % 2)
    if bits & 2:
        row = row + 2 - 4 * ((row // 2) % 2)
    if bits & 4:
        row = row + 4 - 8 * ((row // 4) % 2)
    return row


def whole_kernel(
    total_rows,
    x_hbm,
    v_hbm,
    out_ref,
    own_x,
    turned_x,
    own_v,
    far_x,
    far_v,
    own_norm,
    acc,
    parts,
    plane_gram,
    depth_gram,
    own_sem,
    own_v_sem,
    x_send,
    x_recv,
    v_send,
    v_recv,
    part_send,
    part_recv,
    plane_send,
    plane_recv,
    depth_send,
    depth_recv,
):
    row = lax.axis_index("row")
    col = lax.axis_index("col")
    row_count = plane_gram.shape[0]
    col_count, padded, block_rows = acc.shape
    eig_count = own_v.shape[0]
    half = block_rows // 2
    width = own_x.shape[1]
    mesh_ids = pl.DeviceIdType.MESH

    load = pltpu.make_async_copy(x_hbm, own_x, own_sem)
    load.start()
    load_v = pltpu.make_async_copy(v_hbm, own_v, own_v_sem)
    load_v.start()

    barrier = pltpu.get_barrier_semaphore()
    for bits in range(1, row_count):
        pl.semaphore_signal(barrier, inc=1, device_id=(across(row, bits), col), device_id_type=mesh_ids)
    for step in range(1, col_count):
        pl.semaphore_signal(barrier, inc=1, device_id=(row, (col + step) % col_count), device_id_type=mesh_ids)
    pl.semaphore_wait(barrier, row_count + col_count - 2)

    def unit_copies(source, target, bits):
        if source < 2:
            start = pl.multiple_of(col * block_rows + source * half, half)
            x_src = x_hbm.at[pl.ds(start, half), :]
            v_src = v_hbm.at[:, pl.ds(source * half, half)]
        else:
            x_src = far_x.at[source]
            v_src = far_v.at[source]
        partner = (across(row, bits), col)
        return (
            pltpu.make_async_remote_copy(
                src_ref=v_src, dst_ref=far_v.at[target], send_sem=v_send.at[target],
                recv_sem=v_recv.at[target], device_id=partner, device_id_type=mesh_ids,
            ),
            pltpu.make_async_remote_copy(
                src_ref=x_src, dst_ref=far_x.at[target], send_sem=x_send.at[target],
                recv_sem=x_recv.at[target], device_id=partner, device_id_type=mesh_ids,
            ),
        )

    def start_unit(item):
        for copy in unit_copies(*item):
            copy.start()

    def wait_unit(target):
        pltpu.make_async_copy(far_v.at[target], far_v.at[target], v_recv.at[target]).wait()
        pltpu.make_async_copy(far_x.at[target], far_x.at[target], x_recv.at[target]).wait()

    for item in FIRST_SENDS:
        start_unit(item)

    load.wait()
    load_v.wait()
    far_v[0] = own_v[:, :half]
    far_v[1] = own_v[:, half:]
    for part in range(2):
        start = pl.multiple_of(col * block_rows + part * half, half)
        far_x[part] = own_x[pl.ds(start, half), :]
    acc[...] = jnp.zeros_like(acc)

    @pl.loop(0, col_count)
    def _(near):
        rows = own_x[pl.ds(pl.multiple_of(near * block_rows, block_rows), block_rows), :]
        turned = rows.astype(jnp.float32).T
        turned_x[near] = turned.astype(jnp.bfloat16)
        mean = jnp.sum(turned * turned, axis=0, keepdims=True) * (1.0 / width)
        own_norm[near] = jnp.broadcast_to(lax.rsqrt(mean + 1e-06), (8, block_rows))

    scale = 1.4426950408889634 / math.sqrt(width)

    def pair_norm(unit):
        wide = far_x[pl.ds(unit, 2)].reshape(block_rows, width).astype(jnp.float32)
        mean = jnp.sum(wide * wide, axis=1, keepdims=True) * (1.0 / width)
        return lax.rsqrt(mean + 1e-06) * scale

    def pair_scores(unit, near):
        cols = far_x[pl.ds(unit, 2)].reshape(block_rows, width)
        return jnp.dot(cols, turned_x[near], preferred_element_type=jnp.float32)

    def add_tile(unit, near, scores, col_norm):
        affinity = jnp.exp2(scores * own_norm[near, 0:1, :] * col_norm)
        acc[near, eig_count:, :] += jnp.sum(affinity.reshape(block_rows // 8, 8, block_rows), axis=0)
        cols_v = jnp.concatenate([far_v[unit], far_v[unit + 1]], axis=1)
        acc[near, :eig_count, :] += jnp.dot(
            cols_v, affinity.astype(jnp.bfloat16), preferred_element_type=jnp.float32
        )

    @pl.loop(0, UNITS // 2 - 1)
    def _(pair_at):
        unit = pair_at * 2

        @pl.when(unit == 2)
        def _():
            acc[col] = jnp.zeros((padded, block_rows), jnp.float32)

        for first, items in RELAYS.items():
            @pl.when(unit == first)
            def _(first=first, items=items):
                wait_unit(first)
                wait_unit(first + 1)
                for item in items:
                    start_unit(item)

        for first in (2, 6, 10):
            @pl.when(unit == first)
            def _(first=first):
                wait_unit(first)
                wait_unit(first + 1)

        scores = pair_scores(unit, 0)
        col_norm = pair_norm(unit)
        for near in range(col_count):
            current = scores
            if near + 1 < col_count:
                scores = pair_scores(unit, near + 1)
            add_tile(unit, near, current, col_norm)

    pair = col + 1 - 2 * (col % 2)
    far = (col + 2) % col_count
    far_pair = col_count - 1 - col

    def part_copy(at):
        source, target = ((far_pair, pair), (pair, pair), (far, far))[at]
        return pltpu.make_async_remote_copy(
            src_ref=acc.at[source], dst_ref=parts.at[at], send_sem=part_send.at[at],
            recv_sem=part_recv.at[at], device_id=(row, target), device_id_type=mesh_ids,
        )

    last = UNITS - 2
    wait_unit(last)
    wait_unit(last + 1)
    order = (far_pair, pair, far, col)
    scores = pair_scores(last, order[0])
    last_norm = pair_norm(last)
    for at, near in enumerate(order):
        current = scores
        if at + 1 < col_count:
            scores = pair_scores(last, order[at + 1])
        add_tile(last, near, current, last_norm)
        if at == 2:
            part_copy(0).wait_recv()
            acc[far] = acc[far] + parts[0]
        if at < 3:
            part_copy(at).start()
    part_copy(1).wait_recv()
    part_copy(2).wait_recv()
    total = acc[col] + parts[1] + parts[2]
    degree = jnp.sum(total[eig_count:, :], axis=0, keepdims=True)
    smoothed = total[:eig_count, :] / degree

    def gram_sum(gram, held, me, partners, send_sem, recv_sem):
        held[me] = gram
        copies = []
        for at, partner in enumerate(partners):
            copies.append(
                pltpu.make_async_remote_copy(
                    src_ref=held.at[me], dst_ref=held.at[me], send_sem=send_sem.at[at],
                    recv_sem=recv_sem.at[at], device_id=partner, device_id_type=mesh_ids,
                )
            )
        for copy in copies:
            copy.start()
        for copy in copies:
            copy.wait()
        return jnp.sum(held[...], axis=0)

    gram = lax.dot_general(
        smoothed, smoothed, (((1,), (1,)), ((), ())),
        precision=lax.Precision.HIGHEST, preferred_element_type=jnp.float32,
    )
    packed = jnp.concatenate([gram[: eig_count // 2, :], gram[eig_count // 2 :, :]], axis=1)
    packed = gram_sum(
        packed, plane_gram, row, [(across(row, bits), col) for bits in range(1, row_count)],
        plane_send, plane_recv,
    )
    packed = gram_sum(
        packed, depth_gram, col, [(row, (col + step) % col_count) for step in range(1, col_count)],
        depth_send, depth_recv,
    )
    gram = jnp.concatenate([packed[:, :eig_count], packed[:, eig_count:]], axis=0) / total_rows

    down = lax.broadcasted_iota(jnp.int32, (8, 2 * eig_count), 0)
    at_row = lax.broadcasted_iota(jnp.int32, (eig_count, eig_count), 0)
    at_col = lax.broadcasted_iota(jnp.int32, (eig_count, eig_count), 1)
    diagonal = at_row == at_col
    work = jnp.concatenate([diagonal.astype(jnp.float32), gram], axis=1)
    groups = [work[start : start + 8, :] for start in range(0, eig_count, 8)]
    for step in range(eig_count - 1):
        at, group, inner = eig_count + step, step // 8, step % 8
        column = [
            jnp.broadcast_to(held[:, at : at + 1], (8, 2 * eig_count)) for held in groups[group:]
        ]
        scaled = groups[group][inner : inner + 1, :] / column[0][inner : inner + 1, :]
        column[0] = jnp.where(down > inner, column[0], 0.0)
        for place, values in enumerate(column):
            groups[group + place] = groups[group + place] - values * scaled
    work = jnp.concatenate(groups, axis=0)
    pivots = jnp.sum(jnp.where(diagonal, work[:, eig_count:], 0.0), axis=1, keepdims=True)
    inverse = work[:, :eig_count] * lax.rsqrt(pivots)
    out_ref[...] = jnp.dot(
        inverse, smoothed, precision=lax.Precision.HIGHEST, preferred_element_type=jnp.float32
    )

    for item in FIRST_SENDS + sum(RELAYS.values(), ()):
        for copy in unit_copies(*item):
            copy.wait_send()
    for at in range(3):
        part_copy(at).wait_send()


def per_device_full(total_rows, row_count, embeddings, vectors, block_pairs):
    del block_pairs
    eig_count, block_rows = vectors.shape
    near_rows, width = embeddings.shape
    col_count = near_rows // block_rows
    half = block_rows // 2
    padded = eig_count + 8
    dma = pltpu.SemaphoreType.DMA
    return pl.pallas_call(
        functools.partial(whole_kernel, total_rows),
        out_shape=jax.ShapeDtypeStruct((eig_count, block_rows), jnp.float32),
        in_specs=[pl.BlockSpec(memory_space=pl.ANY)] * 2,
        out_specs=pl.BlockSpec(memory_space=pltpu.VMEM),
        scratch_shapes=[
            pltpu.VMEM((near_rows, width), jnp.bfloat16),
            pltpu.VMEM((col_count, width, block_rows), jnp.bfloat16),
            pltpu.VMEM((eig_count, block_rows), jnp.bfloat16),
            pltpu.VMEM((UNITS, half, width), jnp.bfloat16),
            pltpu.VMEM((UNITS, eig_count, half), jnp.bfloat16),
            pltpu.VMEM((col_count, 8, block_rows), jnp.float32),
            pltpu.VMEM((col_count, padded, block_rows), jnp.float32),
            pltpu.VMEM((col_count - 1, padded, block_rows), jnp.float32),
            pltpu.VMEM((row_count, eig_count // 2, 2 * eig_count), jnp.float32),
            pltpu.VMEM((col_count, eig_count // 2, 2 * eig_count), jnp.float32),
            dma(()),
            dma(()),
            dma((UNITS,)),
            dma((UNITS,)),
            dma((UNITS,)),
            dma((UNITS,)),
            dma((col_count - 1,)),
            dma((col_count - 1,)),
            dma((row_count - 1,)),
            dma((row_count - 1,)),
            dma((col_count - 1,)),
            dma((col_count - 1,)),
        ],
        compiler_params=pltpu.CompilerParams(
            collective_id=0, has_side_effects=True, vmem_limit_bytes=60 * 1024 * 1024
        ),
    )(embeddings, vectors)


def solution(mesh):
    row_count, col_count = mesh.shape["row"], mesh.shape["col"]

    def step(embeddings, vectors, block_pairs):
        blocks = row_count * col_count
        full = block_pairs.shape[0] == blocks * (blocks - 1) and (row_count, col_count) == (8, 4)
        body = per_device
        if full:
            body = functools.partial(per_device_full, embeddings.shape[0], row_count)
        return jax.shard_map(
            body,
            mesh=mesh,
            in_specs=(P("row", None), P(None, ("row", "col")), P()),
            out_specs=P(None, ("row", "col")),
            check_vma=False,
        )(embeddings, vectors, block_pairs)

    return step
```

```python
import functools
import math

import jax
import jax.numpy as jnp
from jax import lax
from jax.experimental import pallas as pl
from jax.experimental.pallas import tpu as pltpu
from jax.sharding import PartitionSpec as P


def inverse_norms(blocks):
    return lax.rsqrt(jnp.mean(jnp.square(blocks.astype(jnp.float32)), axis=-1) + 1e-06)


def tile_terms(rows_x, cols_x, norm_rows, norm_cols, cols_v, feature_width):
    scores = jnp.dot(rows_x, cols_x.T, preferred_element_type=jnp.float32)
    affinity = jnp.exp(scores * norm_rows[:, None] * norm_cols[None, :] / math.sqrt(feature_width))
    rounded = affinity.astype(jnp.bfloat16)
    contrib = jnp.dot(cols_v, rounded.T, preferred_element_type=jnp.float32)
    return (contrib, jnp.sum(affinity, axis=1))


def tile_mask(block_pairs, near_column, col_count, row_count, here_row, here_col):
    near_ids = block_pairs[:, near_column]
    far_ids = block_pairs[:, 1 - near_column]
    member = (near_ids // col_count == here_row) & (far_ids % col_count == here_col)
    near_hot = ((near_ids % col_count)[:, None] == jnp.arange(col_count)[None, :]) & member[:, None]
    far_hot = (far_ids // col_count)[:, None] == jnp.arange(row_count)[None, :]
    return jnp.dot(
        near_hot.astype(jnp.float32).T,
        far_hot.astype(jnp.float32),
        preferred_element_type=jnp.float32,
    )


def add_block(running, contrib, row_totals, column_start, block_rows):
    sums_now, degree_now = running
    old_sums = lax.dynamic_slice_in_dim(sums_now, column_start, block_rows, 1)
    sums_now = lax.dynamic_update_slice_in_dim(sums_now, old_sums + contrib, column_start, 1)
    old_degree = lax.dynamic_slice_in_dim(degree_now, column_start, block_rows, 1)
    degree_now = lax.dynamic_update_slice_in_dim(
        degree_now, old_degree + row_totals[None, :], column_start, 1
    )
    return (sums_now, degree_now)


def per_device(embeddings, vectors, block_pairs):
    col_count = lax.axis_size("col")
    row_count = lax.axis_size("row")
    here_row = lax.axis_index("row")
    here_col = lax.axis_index("col")
    eig_count, block_rows = vectors.shape
    feature_width = embeddings.shape[1]
    near_blocks = embeddings.reshape(col_count, block_rows, feature_width)
    near_norms = inverse_norms(near_blocks)
    own_block = lax.dynamic_slice_in_dim(near_blocks, here_col, 1, 0)
    present = tile_mask(block_pairs, 0, col_count, row_count, here_row, here_col)
    start_sums = jnp.zeros((eig_count, col_count * block_rows), jnp.float32)
    start_degree = jnp.zeros((1, col_count * block_rows), jnp.float32)
    far_x = lax.all_gather(own_block, "row", axis=0, tiled=True)
    far_v = lax.all_gather(vectors[None], "row", axis=0, tiled=True)
    far_norms = inverse_norms(far_x)
    piece_blocks = far_x.shape[0]

    def visit(position, current):
        far_index = position // col_count
        near_index = position % col_count

        def compute(totals):
            contrib, row_totals = tile_terms(
                near_blocks[near_index],
                far_x[far_index],
                near_norms[near_index],
                far_norms[far_index],
                far_v[far_index],
                feature_width,
            )
            return add_block(totals, contrib, row_totals, near_index * block_rows, block_rows)

        return lax.cond(
            present[near_index, far_index] > 0.5, compute, lambda totals: totals, current
        )

    partial_sums, degree = lax.fori_loop(
        0, piece_blocks * col_count, visit, (start_sums, start_degree)
    )
    owned_sums, owned_degree = (
        lax.psum_scatter(partial_sums, "col", scatter_dimension=1, tiled=True),
        lax.psum_scatter(degree, "col", scatter_dimension=1, tiled=True),
    )
    smoothed = owned_sums / owned_degree
    total_rows = block_rows * col_count * row_count
    local_gram = jnp.dot(
        smoothed, smoothed.T, precision=lax.Precision.HIGHEST, preferred_element_type=jnp.float32
    )
    gram_matrix = lax.psum(local_gram, ("row", "col")) / total_rows
    factor = jnp.linalg.cholesky(gram_matrix)
    return lax.linalg.triangular_solve(factor, smoothed, left_side=True, lower=True)


UNITS = 16
FIRST_SENDS = ((0, 4, 2), (1, 5, 4), (0, 2, 1), (1, 3, 1), (1, 8, 2), (0, 9, 4))
RELAYS = {
    4: ((4, 12, 4), (5, 13, 2), (4, 6, 1), (5, 7, 1)),
    8: ((8, 10, 1), (9, 11, 1)),
    12: ((12, 14, 1), (13, 15, 1)),
}


def across(row, bits):
    if bits & 1:
        row = row + 1 - 2 * (row % 2)
    if bits & 2:
        row = row + 2 - 4 * ((row // 2) % 2)
    if bits & 4:
        row = row + 4 - 8 * ((row // 4) % 2)
    return row


def whole_kernel(
    total_rows,
    x_hbm,
    v_hbm,
    out_ref,
    own_x,
    turned_x,
    own_v,
    far_x,
    far_v,
    own_norm,
    acc,
    parts,
    plane_gram,
    depth_gram,
    own_sem,
    own_v_sem,
    x_send,
    x_recv,
    v_send,
    v_recv,
    part_send,
    part_recv,
    plane_send,
    plane_recv,
    depth_send,
    depth_recv,
):
    row = lax.axis_index("row")
    col = lax.axis_index("col")
    row_count = plane_gram.shape[0]
    col_count, padded, block_rows = acc.shape
    eig_count = own_v.shape[0]
    half = block_rows // 2
    quarter = half // 2
    width = own_x.shape[1]
    mesh_ids = pl.DeviceIdType.MESH

    load = pltpu.make_async_copy(x_hbm, own_x, own_sem)
    load.start()
    load_v = pltpu.make_async_copy(v_hbm, own_v, own_v_sem)
    load_v.start()

    barrier = pltpu.get_barrier_semaphore()
    for bits in range(1, row_count):
        pl.semaphore_signal(barrier, inc=1, device_id=(across(row, bits), col), device_id_type=mesh_ids)
    for step in range(1, col_count):
        pl.semaphore_signal(barrier, inc=1, device_id=(row, (col + step) % col_count), device_id_type=mesh_ids)
    pl.semaphore_wait(barrier, row_count + col_count - 2)

    def unit_copies(source, target, bits):
        if source < 2:
            start = pl.multiple_of(col * block_rows + source * half, half)
            x_src = [x_hbm.at[pl.ds(start + at * quarter, quarter), :] for at in range(2)]
            v_src = v_hbm.at[:, pl.ds(source * half, half)]
        else:
            x_src = [far_x.at[source, pl.ds(at * quarter, quarter), :] for at in range(2)]
            v_src = far_v.at[source]
        partner = (across(row, bits), col)
        return (
            pltpu.make_async_remote_copy(
                src_ref=v_src, dst_ref=far_v.at[target], send_sem=v_send.at[target],
                recv_sem=v_recv.at[target], device_id=partner, device_id_type=mesh_ids,
            ),
        ) + tuple(
            pltpu.make_async_remote_copy(
                src_ref=x_src[at], dst_ref=far_x.at[target, pl.ds(at * quarter, quarter), :],
                send_sem=x_send.at[at, target], recv_sem=x_recv.at[at, target],
                device_id=partner, device_id_type=mesh_ids,
            )
            for at in range(2)
        )

    def start_unit(item):
        for copy in unit_copies(*item):
            copy.start()

    def wait_unit(target):
        pltpu.make_async_copy(far_v.at[target], far_v.at[target], v_recv.at[target]).wait()
        for at in range(2):
            piece = far_x.at[target, pl.ds(at * quarter, quarter), :]
            pltpu.make_async_copy(piece, piece, x_recv.at[at, target]).wait()

    for item in FIRST_SENDS:
        start_unit(item)

    load.wait()
    load_v.wait()
    far_v[0] = own_v[:, :half]
    far_v[1] = own_v[:, half:]
    for part in range(2):
        start = pl.multiple_of(col * block_rows + part * half, half)
        far_x[part] = own_x[pl.ds(start, half), :]
    acc[...] = jnp.zeros_like(acc)

    @pl.loop(0, col_count)
    def _(near):
        rows = own_x[pl.ds(pl.multiple_of(near * block_rows, block_rows), block_rows), :]
        turned = rows.astype(jnp.float32).T
        turned_x[near] = turned.astype(jnp.bfloat16)
        mean = jnp.sum(turned * turned, axis=0, keepdims=True) * (1.0 / width)
        own_norm[near] = jnp.broadcast_to(lax.rsqrt(mean + 1e-06), (8, block_rows))

    scale = 1.4426950408889634 / math.sqrt(width)

    def pair_norm(unit):
        wide = far_x[pl.ds(unit, 2)].reshape(block_rows, width).astype(jnp.float32)
        mean = jnp.sum(wide * wide, axis=1, keepdims=True) * (1.0 / width)
        return lax.rsqrt(mean + 1e-06) * scale

    def pair_scores(unit, near):
        cols = far_x[pl.ds(unit, 2)].reshape(block_rows, width)
        return jnp.dot(cols, turned_x[near], preferred_element_type=jnp.float32)

    def add_tile(unit, near, scores, col_norm):
        affinity = jnp.exp2(scores * own_norm[near, 0:1, :] * col_norm)
        acc[near, eig_count:, :] += jnp.sum(affinity.reshape(block_rows // 8, 8, block_rows), axis=0)
        cols_v = jnp.concatenate([far_v[unit], far_v[unit + 1]], axis=1)
        acc[near, :eig_count, :] += jnp.dot(
            cols_v, affinity.astype(jnp.bfloat16), preferred_element_type=jnp.float32
        )

    @pl.loop(0, UNITS // 2 - 1)
    def _(pair_at):
        unit = pair_at * 2

        @pl.when(unit == 2)
        def _():
            acc[col] = jnp.zeros((padded, block_rows), jnp.float32)

        for first, items in RELAYS.items():
            @pl.when(unit == first)
            def _(first=first, items=items):
                wait_unit(first)
                wait_unit(first + 1)
                for item in items:
                    start_unit(item)

        for first in (2, 6, 10):
            @pl.when(unit == first)
            def _(first=first):
                wait_unit(first)
                wait_unit(first + 1)

        scores = pair_scores(unit, 0)
        col_norm = pair_norm(unit)
        for near in range(col_count):
            current = scores
            if near + 1 < col_count:
                scores = pair_scores(unit, near + 1)
            add_tile(unit, near, current, col_norm)

    pair = col + 1 - 2 * (col % 2)
    far = (col + 2) % col_count
    far_pair = col_count - 1 - col

    def part_copy(at):
        source, target = ((far_pair, pair), (pair, pair), (far, far))[at]
        return pltpu.make_async_remote_copy(
            src_ref=acc.at[source], dst_ref=parts.at[at], send_sem=part_send.at[at],
            recv_sem=part_recv.at[at], device_id=(row, target), device_id_type=mesh_ids,
        )

    last = UNITS - 2
    wait_unit(last)
    wait_unit(last + 1)
    order = (far_pair, pair, far, col)
    scores = pair_scores(last, order[0])
    last_norm = pair_norm(last)
    for at, near in enumerate(order):
        current = scores
        if at + 1 < col_count:
            scores = pair_scores(last, order[at + 1])
        add_tile(last, near, current, last_norm)
        if at == 2:
            part_copy(0).wait_recv()
            part_copy(1).start()
            acc[far] = acc[far] + parts[0]
            part_copy(2).start()
        if at == 0:
            part_copy(0).start()
    part_copy(1).wait_recv()
    part_copy(2).wait_recv()
    total = acc[col] + parts[1] + parts[2]
    degree = jnp.sum(total[eig_count:, :], axis=0, keepdims=True)
    smoothed = total[:eig_count, :] / degree

    def gram_sum(gram, held, me, partners, send_sem, recv_sem):
        held[me] = gram
        copies = []
        for at, partner in enumerate(partners):
            copies.append(
                pltpu.make_async_remote_copy(
                    src_ref=held.at[me], dst_ref=held.at[me], send_sem=send_sem.at[at],
                    recv_sem=recv_sem.at[at], device_id=partner, device_id_type=mesh_ids,
                )
            )
        for copy in copies:
            copy.start()
        for copy in copies:
            copy.wait()
        return jnp.sum(held[...], axis=0)

    gram = lax.dot_general(
        smoothed, smoothed, (((1,), (1,)), ((), ())),
        precision=lax.Precision.HIGHEST, preferred_element_type=jnp.float32,
    )
    packed = jnp.concatenate([gram[: eig_count // 2, :], gram[eig_count // 2 :, :]], axis=1)
    packed = gram_sum(
        packed, plane_gram, row, [(across(row, bits), col) for bits in range(1, row_count)],
        plane_send, plane_recv,
    )
    packed = gram_sum(
        packed, depth_gram, col, [(row, (col + step) % col_count) for step in range(1, col_count)],
        depth_send, depth_recv,
    )
    gram = jnp.concatenate([packed[:, :eig_count], packed[:, eig_count:]], axis=0) / total_rows

    down = lax.broadcasted_iota(jnp.int32, (8, 2 * eig_count), 0)
    at_row = lax.broadcasted_iota(jnp.int32, (eig_count, eig_count), 0)
    at_col = lax.broadcasted_iota(jnp.int32, (eig_count, eig_count), 1)
    diagonal = at_row == at_col
    work = jnp.concatenate([diagonal.astype(jnp.float32), gram], axis=1)
    groups = [work[start : start + 8, :] for start in range(0, eig_count, 8)]
    for step in range(eig_count - 1):
        at, group, inner = eig_count + step, step // 8, step % 8
        column = [
            jnp.broadcast_to(held[:, at : at + 1], (8, 2 * eig_count)) for held in groups[group:]
        ]
        scaled = groups[group][inner : inner + 1, :] / column[0][inner : inner + 1, :]
        column[0] = jnp.where(down > inner, column[0], 0.0)
        for place, values in enumerate(column):
            groups[group + place] = groups[group + place] - values * scaled
    work = jnp.concatenate(groups, axis=0)
    pivots = jnp.sum(jnp.where(diagonal, work[:, eig_count:], 0.0), axis=1, keepdims=True)
    inverse = work[:, :eig_count] * lax.rsqrt(pivots)
    out_ref[...] = jnp.dot(
        inverse, smoothed, precision=lax.Precision.HIGHEST, preferred_element_type=jnp.float32
    )

    for item in FIRST_SENDS + sum(RELAYS.values(), ()):
        for copy in unit_copies(*item):
            copy.wait_send()
    for at in range(3):
        part_copy(at).wait_send()


def per_device_full(total_rows, row_count, embeddings, vectors, block_pairs):
    del block_pairs
    eig_count, block_rows = vectors.shape
    near_rows, width = embeddings.shape
    col_count = near_rows // block_rows
    half = block_rows // 2
    padded = eig_count + 8
    dma = pltpu.SemaphoreType.DMA
    return pl.pallas_call(
        functools.partial(whole_kernel, total_rows),
        out_shape=jax.ShapeDtypeStruct((eig_count, block_rows), jnp.float32),
        in_specs=[pl.BlockSpec(memory_space=pltpu.HBM)] * 2,
        out_specs=pl.BlockSpec(memory_space=pltpu.VMEM),
        scratch_shapes=[
            pltpu.VMEM((near_rows, width), jnp.bfloat16),
            pltpu.VMEM((col_count, width, block_rows), jnp.bfloat16),
            pltpu.VMEM((eig_count, block_rows), jnp.bfloat16),
            pltpu.VMEM((UNITS, half, width), jnp.bfloat16),
            pltpu.VMEM((UNITS, eig_count, half), jnp.bfloat16),
            pltpu.VMEM((col_count, 8, block_rows), jnp.float32),
            pltpu.VMEM((col_count, padded, block_rows), jnp.float32),
            pltpu.VMEM((col_count - 1, padded, block_rows), jnp.float32),
            pltpu.VMEM((row_count, eig_count // 2, 2 * eig_count), jnp.float32),
            pltpu.VMEM((col_count, eig_count // 2, 2 * eig_count), jnp.float32),
            dma(()),
            dma(()),
            dma((2, UNITS)),
            dma((2, UNITS)),
            dma((UNITS,)),
            dma((UNITS,)),
            dma((col_count - 1,)),
            dma((col_count - 1,)),
            dma((row_count - 1,)),
            dma((row_count - 1,)),
            dma((col_count - 1,)),
            dma((col_count - 1,)),
        ],
        compiler_params=pltpu.CompilerParams(
            collective_id=0, has_side_effects=True, vmem_limit_bytes=48 * 1024 * 1024
        ),
    )(embeddings, vectors)


def solution(mesh):
    row_count, col_count = mesh.shape["row"], mesh.shape["col"]

    def step(embeddings, vectors, block_pairs):
        blocks = row_count * col_count
        full = block_pairs.shape[0] == blocks * (blocks - 1) and (row_count, col_count) == (8, 4)
        body = per_device
        if full:
            body = functools.partial(per_device_full, embeddings.shape[0], row_count)
        return jax.shard_map(
            body,
            mesh=mesh,
            in_specs=(P("row", None), P(None, ("row", "col")), P()),
            out_specs=P(None, ("row", "col")),
            check_vma=False,
        )(embeddings, vectors, block_pairs)

    return step
```

```python
import functools
import math

import jax
import jax.numpy as jnp
from jax import lax
from jax.experimental import pallas as pl
from jax.experimental.pallas import tpu as pltpu
from jax.sharding import PartitionSpec as P


def inverse_norms(blocks):
    return lax.rsqrt(jnp.mean(jnp.square(blocks.astype(jnp.float32)), axis=-1) + 1e-06)


def tile_terms(rows_x, cols_x, norm_rows, norm_cols, cols_v, feature_width):
    scores = jnp.dot(rows_x, cols_x.T, preferred_element_type=jnp.float32)
    affinity = jnp.exp(scores * norm_rows[:, None] * norm_cols[None, :] / math.sqrt(feature_width))
    rounded = affinity.astype(jnp.bfloat16)
    contrib = jnp.dot(cols_v, rounded.T, preferred_element_type=jnp.float32)
    return (contrib, jnp.sum(affinity, axis=1))


def tile_mask(block_pairs, near_column, col_count, row_count, here_row, here_col):
    near_ids = block_pairs[:, near_column]
    far_ids = block_pairs[:, 1 - near_column]
    member = (near_ids // col_count == here_row) & (far_ids % col_count == here_col)
    near_hot = ((near_ids % col_count)[:, None] == jnp.arange(col_count)[None, :]) & member[:, None]
    far_hot = (far_ids // col_count)[:, None] == jnp.arange(row_count)[None, :]
    return jnp.dot(
        near_hot.astype(jnp.float32).T,
        far_hot.astype(jnp.float32),
        preferred_element_type=jnp.float32,
    )


def add_block(running, contrib, row_totals, column_start, block_rows):
    sums_now, degree_now = running
    old_sums = lax.dynamic_slice_in_dim(sums_now, column_start, block_rows, 1)
    sums_now = lax.dynamic_update_slice_in_dim(sums_now, old_sums + contrib, column_start, 1)
    old_degree = lax.dynamic_slice_in_dim(degree_now, column_start, block_rows, 1)
    degree_now = lax.dynamic_update_slice_in_dim(
        degree_now, old_degree + row_totals[None, :], column_start, 1
    )
    return (sums_now, degree_now)


def per_device(embeddings, vectors, block_pairs):
    col_count = lax.axis_size("col")
    row_count = lax.axis_size("row")
    here_row = lax.axis_index("row")
    here_col = lax.axis_index("col")
    eig_count, block_rows = vectors.shape
    feature_width = embeddings.shape[1]
    near_blocks = embeddings.reshape(col_count, block_rows, feature_width)
    near_norms = inverse_norms(near_blocks)
    own_block = lax.dynamic_slice_in_dim(near_blocks, here_col, 1, 0)
    present = tile_mask(block_pairs, 0, col_count, row_count, here_row, here_col)
    start_sums = jnp.zeros((eig_count, col_count * block_rows), jnp.float32)
    start_degree = jnp.zeros((1, col_count * block_rows), jnp.float32)
    far_x = lax.all_gather(own_block, "row", axis=0, tiled=True)
    far_v = lax.all_gather(vectors[None], "row", axis=0, tiled=True)
    far_norms = inverse_norms(far_x)
    piece_blocks = far_x.shape[0]

    def visit(position, current):
        far_index = position // col_count
        near_index = position % col_count

        def compute(totals):
            contrib, row_totals = tile_terms(
                near_blocks[near_index],
                far_x[far_index],
                near_norms[near_index],
                far_norms[far_index],
                far_v[far_index],
                feature_width,
            )
            return add_block(totals, contrib, row_totals, near_index * block_rows, block_rows)

        return lax.cond(
            present[near_index, far_index] > 0.5, compute, lambda totals: totals, current
        )

    partial_sums, degree = lax.fori_loop(
        0, piece_blocks * col_count, visit, (start_sums, start_degree)
    )
    owned_sums, owned_degree = (
        lax.psum_scatter(partial_sums, "col", scatter_dimension=1, tiled=True),
        lax.psum_scatter(degree, "col", scatter_dimension=1, tiled=True),
    )
    smoothed = owned_sums / owned_degree
    total_rows = block_rows * col_count * row_count
    local_gram = jnp.dot(
        smoothed, smoothed.T, precision=lax.Precision.HIGHEST, preferred_element_type=jnp.float32
    )
    gram_matrix = lax.psum(local_gram, ("row", "col")) / total_rows
    factor = jnp.linalg.cholesky(gram_matrix)
    return lax.linalg.triangular_solve(factor, smoothed, left_side=True, lower=True)


UNITS = 16
FIRST_SENDS = ((0, 4, 2), (1, 5, 4), (0, 2, 1), (1, 3, 1), (1, 8, 2), (0, 9, 4))
RELAYS = {
    4: ((4, 12, 4), (5, 13, 2), (4, 6, 1), (5, 7, 1)),
    8: ((8, 10, 1), (9, 11, 1)),
    12: ((12, 14, 1), (13, 15, 1)),
}


def across(row, bits):
    if bits & 1:
        row = row + 1 - 2 * (row % 2)
    if bits & 2:
        row = row + 2 - 4 * ((row // 2) % 2)
    if bits & 4:
        row = row + 4 - 8 * ((row // 4) % 2)
    return row


def whole_kernel(
    total_rows,
    x_hbm,
    v_hbm,
    out_ref,
    own_x,
    turned_x,
    own_v,
    far_x,
    far_v,
    own_norm,
    acc,
    parts,
    plane_gram,
    depth_gram,
    own_sem,
    own_v_sem,
    x_send,
    x_recv,
    v_send,
    v_recv,
    part_send,
    part_recv,
    plane_send,
    plane_recv,
    depth_send,
    depth_recv,
):
    row = lax.axis_index("row")
    col = lax.axis_index("col")
    row_count = plane_gram.shape[0]
    col_count, padded, block_rows = acc.shape
    eig_count = own_v.shape[0]
    half = block_rows // 2
    quarter = half // 2
    width = own_x.shape[1]
    mesh_ids = pl.DeviceIdType.MESH

    load = pltpu.make_async_copy(x_hbm, own_x, own_sem)
    load.start()
    load_v = pltpu.make_async_copy(v_hbm, own_v, own_v_sem)
    load_v.start()

    barrier = pltpu.get_barrier_semaphore()
    for bits in range(1, row_count):
        pl.semaphore_signal(barrier, inc=1, device_id=(across(row, bits), col), device_id_type=mesh_ids)
    for step in range(1, col_count):
        pl.semaphore_signal(barrier, inc=1, device_id=(row, (col + step) % col_count), device_id_type=mesh_ids)
    pl.semaphore_wait(barrier, row_count + col_count - 2)

    def unit_copies(source, target, bits):
        if source < 2:
            start = pl.multiple_of(col * block_rows + source * half, half)
            x_src = [x_hbm.at[pl.ds(start + at * quarter, quarter), :] for at in range(2)]
            v_src = v_hbm.at[:, pl.ds(source * half, half)]
        else:
            x_src = [far_x.at[source, pl.ds(at * quarter, quarter), :] for at in range(2)]
            v_src = far_v.at[source]
        partner = (across(row, bits), col)
        return (
            pltpu.make_async_remote_copy(
                src_ref=v_src, dst_ref=far_v.at[target], send_sem=v_send.at[target],
                recv_sem=v_recv.at[target], device_id=partner, device_id_type=mesh_ids,
            ),
        ) + tuple(
            pltpu.make_async_remote_copy(
                src_ref=x_src[at], dst_ref=far_x.at[target, pl.ds(at * quarter, quarter), :],
                send_sem=x_send.at[at, target], recv_sem=x_recv.at[at, target],
                device_id=partner, device_id_type=mesh_ids,
            )
            for at in range(2)
        )

    def start_unit(item):
        for copy in unit_copies(*item):
            copy.start()

    def wait_unit(target):
        pltpu.make_async_copy(far_v.at[target], far_v.at[target], v_recv.at[target]).wait()
        for at in range(2):
            piece = far_x.at[target, pl.ds(at * quarter, quarter), :]
            pltpu.make_async_copy(piece, piece, x_recv.at[at, target]).wait()

    for item in FIRST_SENDS:
        start_unit(item)

    load.wait()
    load_v.wait()
    far_v[0] = own_v[:, :half]
    far_v[1] = own_v[:, half:]
    for part in range(2):
        start = pl.multiple_of(col * block_rows + part * half, half)
        far_x[part] = own_x[pl.ds(start, half), :]
    acc[...] = jnp.zeros_like(acc)

    @pl.loop(0, col_count)
    def _(near):
        rows = own_x[pl.ds(pl.multiple_of(near * block_rows, block_rows), block_rows), :]
        turned = rows.astype(jnp.float32).T
        turned_x[near] = turned.astype(jnp.bfloat16)
        mean = jnp.sum(turned * turned, axis=0, keepdims=True) * (1.0 / width)
        own_norm[near] = jnp.broadcast_to(lax.rsqrt(mean + 1e-06), (8, block_rows))

    scale = 1.4426950408889634 / math.sqrt(width)

    def pair_norm(unit):
        wide = far_x[pl.ds(unit, 2)].reshape(block_rows, width).astype(jnp.float32)
        mean = jnp.sum(wide * wide, axis=1, keepdims=True) * (1.0 / width)
        return lax.rsqrt(mean + 1e-06) * scale

    def pair_scores(unit, near):
        cols = far_x[pl.ds(unit, 2)].reshape(block_rows, width)
        return jnp.dot(cols, turned_x[near], preferred_element_type=jnp.float32)

    def add_tile(unit, near, scores, col_norm):
        affinity = jnp.exp2(scores * own_norm[near, 0:1, :] * col_norm)
        acc[near, eig_count:, :] += jnp.sum(affinity.reshape(block_rows // 8, 8, block_rows), axis=0)
        cols_v = jnp.concatenate([far_v[unit], far_v[unit + 1]], axis=1)
        acc[near, :eig_count, :] += jnp.dot(
            cols_v, affinity.astype(jnp.bfloat16), preferred_element_type=jnp.float32
        )

    @pl.loop(0, UNITS // 2 - 1)
    def _(pair_at):
        unit = pair_at * 2

        @pl.when(unit == 2)
        def _():
            acc[col] = jnp.zeros((padded, block_rows), jnp.float32)

        for first, items in RELAYS.items():
            @pl.when(unit == first)
            def _(first=first, items=items):
                wait_unit(first)
                wait_unit(first + 1)
                for item in items:
                    start_unit(item)

        for first in (2, 6, 10):
            @pl.when(unit == first)
            def _(first=first):
                wait_unit(first)
                wait_unit(first + 1)

        scores = pair_scores(unit, 0)
        col_norm = pair_norm(unit)
        for near in range(col_count):
            current = scores
            if near + 1 < col_count:
                scores = pair_scores(unit, near + 1)
            add_tile(unit, near, current, col_norm)

    pair = col + 1 - 2 * (col % 2)
    far = (col + 2) % col_count
    far_pair = col_count - 1 - col

    split = eig_count // 2 + 8
    pieces = (pl.ds(0, split), pl.ds(split, padded - split))

    def part_copy(at, piece):
        source, target = ((far_pair, pair), (pair, pair), (far, far))[at]
        rows = pieces[piece]
        return pltpu.make_async_remote_copy(
            src_ref=acc.at[source, rows, :], dst_ref=parts.at[at, rows, :],
            send_sem=part_send.at[piece, at], recv_sem=part_recv.at[piece, at],
            device_id=(row, target), device_id_type=mesh_ids,
        )

    last = UNITS - 2
    wait_unit(last)
    wait_unit(last + 1)
    order = (far_pair, pair, far, col)
    scores = pair_scores(last, order[0])
    last_norm = pair_norm(last)
    for at, near in enumerate(order):
        current = scores
        if at + 1 < col_count:
            scores = pair_scores(last, order[at + 1])
        add_tile(last, near, current, last_norm)
        if at == 0:
            part_copy(0, 0).start()
            part_copy(0, 1).start()
        if at == 2:
            for piece, rows in enumerate(pieces):
                part_copy(0, piece).wait_recv()
                acc[far, rows, :] = acc[far, rows, :] + parts[0, rows, :]
                part_copy(2, piece).start()
                part_copy(1, piece).start()
    for at in (1, 2):
        for piece in range(2):
            part_copy(at, piece).wait_recv()
    total = acc[col] + parts[1] + parts[2]
    degree = jnp.sum(total[eig_count:, :], axis=0, keepdims=True)
    smoothed = total[:eig_count, :] / degree

    def gram_sum(gram, held, me, partners, send_sem, recv_sem):
        held[me] = gram
        copies = []
        for at, partner in enumerate(partners):
            copies.append(
                pltpu.make_async_remote_copy(
                    src_ref=held.at[me], dst_ref=held.at[me], send_sem=send_sem.at[at],
                    recv_sem=recv_sem.at[at], device_id=partner, device_id_type=mesh_ids,
                )
            )
        for copy in copies:
            copy.start()
        for copy in copies:
            copy.wait()
        return jnp.sum(held[...], axis=0)

    gram = lax.dot_general(
        smoothed, smoothed, (((1,), (1,)), ((), ())),
        precision=lax.Precision.HIGHEST, preferred_element_type=jnp.float32,
    )
    packed = jnp.concatenate([gram[: eig_count // 2, :], gram[eig_count // 2 :, :]], axis=1)
    packed = gram_sum(
        packed, plane_gram, row, [(across(row, bits), col) for bits in range(1, row_count)],
        plane_send, plane_recv,
    )
    packed = gram_sum(
        packed, depth_gram, col, [(row, (col + step) % col_count) for step in range(1, col_count)],
        depth_send, depth_recv,
    )
    gram = jnp.concatenate([packed[:, :eig_count], packed[:, eig_count:]], axis=0) / total_rows

    down = lax.broadcasted_iota(jnp.int32, (8, 2 * eig_count), 0)
    at_row = lax.broadcasted_iota(jnp.int32, (eig_count, eig_count), 0)
    at_col = lax.broadcasted_iota(jnp.int32, (eig_count, eig_count), 1)
    diagonal = at_row == at_col
    work = jnp.concatenate([diagonal.astype(jnp.float32), gram], axis=1)
    groups = [work[start : start + 8, :] for start in range(0, eig_count, 8)]
    def spread(held, at):
        return jnp.broadcast_to(held[:, at : at + 1], (8, 2 * eig_count))

    for step in range(0, eig_count, 2):
        at, group, inner = eig_count + step, step // 8, step % 8
        first = [spread(held, at) for held in groups[group:]]
        second = [spread(held, at + 1) for held in groups[group:]]
        upper = groups[group][inner : inner + 1, :]
        lower = groups[group][inner + 1 : inner + 2, :]
        top = 1.0 / first[0][inner : inner + 1, :]
        side = second[0][inner : inner + 1, :] * top
        cross = first[0][inner + 1 : inner + 2, :]
        lower = lower - cross * top * upper
        bottom = 1.0 / (second[0][inner + 1 : inner + 2, :] - cross * side)
        upper, lower = upper * top, lower * bottom
        for place in range(len(first)):
            one, two = first[place], second[place] - first[place] * side
            if place == 0:
                one, two = jnp.where(down > inner, one, 0.0), jnp.where(down > inner + 1, two, 0.0)
            groups[group + place] = groups[group + place] - one * upper - two * lower
    work = jnp.concatenate(groups, axis=0)
    pivots = jnp.sum(jnp.where(diagonal, work[:, eig_count:], 0.0), axis=1, keepdims=True)
    inverse = work[:, :eig_count] * lax.rsqrt(pivots)
    out_ref[...] = jnp.dot(
        inverse, smoothed, precision=lax.Precision.HIGHEST, preferred_element_type=jnp.float32
    )

    for item in FIRST_SENDS + sum(RELAYS.values(), ()):
        for copy in unit_copies(*item):
            copy.wait_send()
    for at in range(3):
        for piece in range(2):
            part_copy(at, piece).wait_send()


def per_device_full(total_rows, row_count, embeddings, vectors, block_pairs):
    del block_pairs
    eig_count, block_rows = vectors.shape
    near_rows, width = embeddings.shape
    col_count = near_rows // block_rows
    half = block_rows // 2
    padded = eig_count + 8
    dma = pltpu.SemaphoreType.DMA
    return pl.pallas_call(
        functools.partial(whole_kernel, total_rows),
        out_shape=jax.ShapeDtypeStruct((eig_count, block_rows), jnp.float32),
        in_specs=[pl.BlockSpec(memory_space=pl.ANY)] * 2,
        out_specs=pl.BlockSpec(memory_space=pltpu.VMEM),
        scratch_shapes=[
            pltpu.VMEM((near_rows, width), jnp.bfloat16),
            pltpu.VMEM((col_count, width, block_rows), jnp.bfloat16),
            pltpu.VMEM((eig_count, block_rows), jnp.bfloat16),
            pltpu.VMEM((UNITS, half, width), jnp.bfloat16),
            pltpu.VMEM((UNITS, eig_count, half), jnp.bfloat16),
            pltpu.VMEM((col_count, 8, block_rows), jnp.float32),
            pltpu.VMEM((col_count, padded, block_rows), jnp.float32),
            pltpu.VMEM((col_count - 1, padded, block_rows), jnp.float32),
            pltpu.VMEM((row_count, eig_count // 2, 2 * eig_count), jnp.float32),
            pltpu.VMEM((col_count, eig_count // 2, 2 * eig_count), jnp.float32),
            dma(()),
            dma(()),
            dma((2, UNITS)),
            dma((2, UNITS)),
            dma((UNITS,)),
            dma((UNITS,)),
            dma((2, col_count - 1)),
            dma((2, col_count - 1)),
            dma((row_count - 1,)),
            dma((row_count - 1,)),
            dma((col_count - 1,)),
            dma((col_count - 1,)),
        ],
        compiler_params=pltpu.CompilerParams(
            collective_id=0, has_side_effects=True, vmem_limit_bytes=60 * 1024 * 1024
        ),
    )(embeddings, vectors)


def solution(mesh):
    row_count, col_count = mesh.shape["row"], mesh.shape["col"]

    def step(embeddings, vectors, block_pairs):
        blocks = row_count * col_count
        full = block_pairs.shape[0] == blocks * (blocks - 1) and (row_count, col_count) == (8, 4)
        body = per_device
        if full:
            body = functools.partial(per_device_full, embeddings.shape[0], row_count)
        return jax.shard_map(
            body,
            mesh=mesh,
            in_specs=(P("row", None), P(None, ("row", "col")), P()),
            out_specs=P(None, ("row", "col")),
            check_vma=False,
        )(embeddings, vectors, block_pairs)

    return step
```

```python
import functools
import math

import jax
import jax.numpy as jnp
from jax import lax
from jax.experimental import pallas as pl
from jax.experimental.pallas import tpu as pltpu
from jax.sharding import PartitionSpec as P


def inverse_norms(blocks):
    return lax.rsqrt(jnp.mean(jnp.square(blocks.astype(jnp.float32)), axis=-1) + 1e-06)


def tile_terms(rows_x, cols_x, norm_rows, norm_cols, cols_v, feature_width):
    scores = jnp.dot(rows_x, cols_x.T, preferred_element_type=jnp.float32)
    affinity = jnp.exp(scores * norm_rows[:, None] * norm_cols[None, :] / math.sqrt(feature_width))
    rounded = affinity.astype(jnp.bfloat16)
    contrib = jnp.dot(cols_v, rounded.T, preferred_element_type=jnp.float32)
    return (contrib, jnp.sum(affinity, axis=1))


def tile_mask(block_pairs, near_column, col_count, row_count, here_row, here_col):
    near_ids = block_pairs[:, near_column]
    far_ids = block_pairs[:, 1 - near_column]
    member = (near_ids // col_count == here_row) & (far_ids % col_count == here_col)
    near_hot = ((near_ids % col_count)[:, None] == jnp.arange(col_count)[None, :]) & member[:, None]
    far_hot = (far_ids // col_count)[:, None] == jnp.arange(row_count)[None, :]
    return jnp.dot(
        near_hot.astype(jnp.float32).T,
        far_hot.astype(jnp.float32),
        preferred_element_type=jnp.float32,
    )


def add_block(running, contrib, row_totals, column_start, block_rows):
    sums_now, degree_now = running
    old_sums = lax.dynamic_slice_in_dim(sums_now, column_start, block_rows, 1)
    sums_now = lax.dynamic_update_slice_in_dim(sums_now, old_sums + contrib, column_start, 1)
    old_degree = lax.dynamic_slice_in_dim(degree_now, column_start, block_rows, 1)
    degree_now = lax.dynamic_update_slice_in_dim(
        degree_now, old_degree + row_totals[None, :], column_start, 1
    )
    return (sums_now, degree_now)


def per_device(embeddings, vectors, block_pairs):
    col_count = lax.axis_size("col")
    row_count = lax.axis_size("row")
    here_row = lax.axis_index("row")
    here_col = lax.axis_index("col")
    eig_count, block_rows = vectors.shape
    feature_width = embeddings.shape[1]
    near_blocks = embeddings.reshape(col_count, block_rows, feature_width)
    near_norms = inverse_norms(near_blocks)
    own_block = lax.dynamic_slice_in_dim(near_blocks, here_col, 1, 0)
    present = tile_mask(block_pairs, 0, col_count, row_count, here_row, here_col)
    start_sums = jnp.zeros((eig_count, col_count * block_rows), jnp.float32)
    start_degree = jnp.zeros((1, col_count * block_rows), jnp.float32)
    far_x = lax.all_gather(own_block, "row", axis=0, tiled=True)
    far_v = lax.all_gather(vectors[None], "row", axis=0, tiled=True)
    far_norms = inverse_norms(far_x)
    piece_blocks = far_x.shape[0]

    def visit(position, current):
        far_index = position // col_count
        near_index = position % col_count

        def compute(totals):
            contrib, row_totals = tile_terms(
                near_blocks[near_index],
                far_x[far_index],
                near_norms[near_index],
                far_norms[far_index],
                far_v[far_index],
                feature_width,
            )
            return add_block(totals, contrib, row_totals, near_index * block_rows, block_rows)

        return lax.cond(
            present[near_index, far_index] > 0.5, compute, lambda totals: totals, current
        )

    partial_sums, degree = lax.fori_loop(
        0, piece_blocks * col_count, visit, (start_sums, start_degree)
    )
    owned_sums, owned_degree = (
        lax.psum_scatter(partial_sums, "col", scatter_dimension=1, tiled=True),
        lax.psum_scatter(degree, "col", scatter_dimension=1, tiled=True),
    )
    smoothed = owned_sums / owned_degree
    total_rows = block_rows * col_count * row_count
    local_gram = jnp.dot(
        smoothed, smoothed.T, precision=lax.Precision.HIGHEST, preferred_element_type=jnp.float32
    )
    gram_matrix = lax.psum(local_gram, ("row", "col")) / total_rows
    factor = jnp.linalg.cholesky(gram_matrix)
    return lax.linalg.triangular_solve(factor, smoothed, left_side=True, lower=True)


UNITS = 16
FIRST_SENDS = ((0, 4, 2), (1, 5, 4), (0, 2, 1), (1, 3, 1), (1, 8, 2), (0, 9, 4))
RELAYS = {
    4: ((4, 12, 4), (5, 13, 2), (4, 6, 1), (5, 7, 1)),
    8: ((8, 10, 1), (9, 11, 1)),
    12: ((12, 14, 1), (13, 15, 1)),
}


def across(row, bits):
    if bits & 1:
        row = row + 1 - 2 * (row % 2)
    if bits & 2:
        row = row + 2 - 4 * ((row // 2) % 2)
    if bits & 4:
        row = row + 4 - 8 * ((row // 4) % 2)
    return row


def whole_kernel(
    total_rows,
    x_hbm,
    v_hbm,
    out_ref,
    own_x,
    turned_x,
    own_v,
    far_x,
    far_v,
    own_norm,
    acc,
    parts,
    plane_gram,
    depth_gram,
    own_sem,
    own_v_sem,
    x_send,
    x_recv,
    v_send,
    v_recv,
    part_send,
    part_recv,
    plane_send,
    plane_recv,
    depth_send,
    depth_recv,
):
    row = lax.axis_index("row")
    col = lax.axis_index("col")
    row_count = plane_gram.shape[0]
    col_count, padded, block_rows = acc.shape
    eig_count = own_v.shape[0]
    half = block_rows // 2
    quarter = half // 2
    width = own_x.shape[1]
    mesh_ids = pl.DeviceIdType.MESH

    load = pltpu.make_async_copy(x_hbm, own_x, own_sem)
    load.start()
    load_v = pltpu.make_async_copy(v_hbm, own_v, own_v_sem)
    load_v.start()

    barrier = pltpu.get_barrier_semaphore()
    for bits in range(1, row_count):
        pl.semaphore_signal(barrier, inc=1, device_id=(across(row, bits), col), device_id_type=mesh_ids)
    for step in range(1, col_count):
        pl.semaphore_signal(barrier, inc=1, device_id=(row, (col + step) % col_count), device_id_type=mesh_ids)
    pl.semaphore_wait(barrier, row_count + col_count - 2)

    def unit_copies(source, target, bits):
        if source < 2:
            start = pl.multiple_of(col * block_rows + source * half, half)
            x_src = [x_hbm.at[pl.ds(start + at * quarter, quarter), :] for at in range(2)]
            v_src = v_hbm.at[:, pl.ds(source * half, half)]
        else:
            x_src = [far_x.at[source, pl.ds(at * quarter, quarter), :] for at in range(2)]
            v_src = far_v.at[source]
        partner = (across(row, bits), col)
        return (
            pltpu.make_async_remote_copy(
                src_ref=v_src, dst_ref=far_v.at[target], send_sem=v_send.at[target],
                recv_sem=v_recv.at[target], device_id=partner, device_id_type=mesh_ids,
            ),
        ) + tuple(
            pltpu.make_async_remote_copy(
                src_ref=x_src[at], dst_ref=far_x.at[target, pl.ds(at * quarter, quarter), :],
                send_sem=x_send.at[at, target], recv_sem=x_recv.at[at, target],
                device_id=partner, device_id_type=mesh_ids,
            )
            for at in range(2)
        )

    def start_unit(item):
        for copy in unit_copies(*item):
            copy.start()

    def wait_v(target):
        pltpu.make_async_copy(far_v.at[target], far_v.at[target], v_recv.at[target]).wait()

    def wait_x(target, at):
        piece = far_x.at[target, pl.ds(at * quarter, quarter), :]
        pltpu.make_async_copy(piece, piece, x_recv.at[at, target]).wait()

    def wait_unit(target):
        wait_v(target)
        for at in range(2):
            wait_x(target, at)

    def relay(first):
        copies = [unit_copies(*item) for item in RELAYS[first]]
        wait_v(first)
        wait_v(first + 1)
        for held in copies:
            held[0].start()
        for at in range(2):
            wait_x(first, at)
            wait_x(first + 1, at)
            for held in copies:
                held[1 + at].start()

    for item in FIRST_SENDS:
        start_unit(item)

    load.wait()
    load_v.wait()
    far_v[0] = own_v[:, :half]
    far_v[1] = own_v[:, half:]
    for part in range(2):
        start = pl.multiple_of(col * block_rows + part * half, half)
        far_x[part] = own_x[pl.ds(start, half), :]
    acc[...] = jnp.zeros_like(acc)

    @pl.loop(0, col_count)
    def _(near):
        rows = own_x[pl.ds(pl.multiple_of(near * block_rows, block_rows), block_rows), :]
        turned = rows.astype(jnp.float32).T
        turned_x[near] = turned.astype(jnp.bfloat16)
        mean = jnp.sum(turned * turned, axis=0, keepdims=True) * (1.0 / width)
        own_norm[near] = jnp.broadcast_to(lax.rsqrt(mean + 1e-06), (8, block_rows))

    scale = 1.4426950408889634 / math.sqrt(width)

    def pair_norm(unit):
        wide = far_x[pl.ds(unit, 2)].reshape(block_rows, width).astype(jnp.float32)
        mean = jnp.sum(wide * wide, axis=1, keepdims=True) * (1.0 / width)
        return lax.rsqrt(mean + 1e-06) * scale

    def pair_scores(unit, near):
        cols = far_x[pl.ds(unit, 2)].reshape(block_rows, width)
        return jnp.dot(cols, turned_x[near], preferred_element_type=jnp.float32)

    def add_tile(unit, near, scores, col_norm):
        affinity = jnp.exp2(scores * own_norm[near, 0:1, :] * col_norm)
        acc[near, eig_count:, :] += jnp.sum(affinity.reshape(block_rows // 8, 8, block_rows), axis=0)
        cols_v = jnp.concatenate([far_v[unit], far_v[unit + 1]], axis=1)
        acc[near, :eig_count, :] += jnp.dot(
            cols_v, affinity.astype(jnp.bfloat16), preferred_element_type=jnp.float32
        )

    @pl.loop(0, UNITS // 2 - 2)
    def _(pair_at):
        unit = pair_at * 2

        @pl.when(unit == 2)
        def _():
            acc[col] = jnp.zeros((padded, block_rows), jnp.float32)

        for first in (4, 8):
            @pl.when(unit == first)
            def _(first=first):
                relay(first)

        for first in (2, 6, 10):
            @pl.when(unit == first)
            def _(first=first):
                wait_unit(first)
                wait_unit(first + 1)

        scores = pair_scores(unit, 0)
        col_norm = pair_norm(unit)
        for near in range(col_count):
            current = scores
            if near + 1 < col_count:
                scores = pair_scores(unit, near + 1)
            add_tile(unit, near, current, col_norm)

    pair = col + 1 - 2 * (col % 2)
    far = (col + 2) % col_count
    far_pair = col_count - 1 - col

    split = eig_count // 2 + 8
    pieces = (pl.ds(0, split), pl.ds(split, padded - split))

    def part_copy(at, piece):
        source, target = ((far_pair, pair), (pair, pair), (far, far))[at]
        rows = pieces[piece]
        return pltpu.make_async_remote_copy(
            src_ref=acc.at[source, rows, :], dst_ref=parts.at[at, rows, :],
            send_sem=part_send.at[piece, at], recv_sem=part_recv.at[piece, at],
            device_id=(row, target), device_id_type=mesh_ids,
        )

    last = UNITS - 2
    relay(last - 2)
    norms = {last - 2: pair_norm(last - 2)}

    def add_last(unit, near):
        add_tile(unit, near, pair_scores(unit, near), norms[unit])

    add_last(last - 2, far_pair)
    add_last(last - 2, pair)
    wait_unit(last)
    wait_unit(last + 1)
    norms[last] = pair_norm(last)
    add_last(last, far_pair)
    part_copy(0, 0).start()
    part_copy(0, 1).start()
    for near in (pair, far):
        add_last(last, near)
        if near is pair:
            add_last(last - 2, far)
    for piece, rows in enumerate(pieces):
        part_copy(0, piece).wait_recv()
        acc[far, rows, :] = acc[far, rows, :] + parts[0, rows, :]
        part_copy(2, piece).start()
        part_copy(1, piece).start()
    add_last(last - 2, col)
    add_last(last, col)
    for at in (1, 2):
        for piece in range(2):
            part_copy(at, piece).wait_recv()
    total = acc[col] + parts[1] + parts[2]
    degree = jnp.sum(total[eig_count:, :], axis=0, keepdims=True)
    smoothed = total[:eig_count, :] / degree

    def gram_sum(gram, held, me, partners, send_sem, recv_sem):
        held[me] = gram
        copies = []
        for at, partner in enumerate(partners):
            copies.append(
                pltpu.make_async_remote_copy(
                    src_ref=held.at[me], dst_ref=held.at[me], send_sem=send_sem.at[at],
                    recv_sem=recv_sem.at[at], device_id=partner, device_id_type=mesh_ids,
                )
            )
        for copy in copies:
            copy.start()
        for copy in copies:
            copy.wait()
        return jnp.sum(held[...], axis=0)

    gram = lax.dot_general(
        smoothed, smoothed, (((1,), (1,)), ((), ())),
        precision=lax.Precision.HIGHEST, preferred_element_type=jnp.float32,
    )
    packed = jnp.concatenate([gram[: eig_count // 2, :], gram[eig_count // 2 :, :]], axis=1)
    packed = gram_sum(
        packed, plane_gram, row, [(across(row, bits), col) for bits in range(1, row_count)],
        plane_send, plane_recv,
    )
    packed = gram_sum(
        packed, depth_gram, col, [(row, (col + step) % col_count) for step in range(1, col_count)],
        depth_send, depth_recv,
    )
    gram = jnp.concatenate([packed[:, :eig_count], packed[:, eig_count:]], axis=0) / total_rows

    down = lax.broadcasted_iota(jnp.int32, (8, 2 * eig_count), 0)
    at_row = lax.broadcasted_iota(jnp.int32, (eig_count, eig_count), 0)
    at_col = lax.broadcasted_iota(jnp.int32, (eig_count, eig_count), 1)
    diagonal = at_row == at_col
    work = jnp.concatenate([diagonal.astype(jnp.float32), gram], axis=1)
    groups = [work[start : start + 8, :] for start in range(0, eig_count, 8)]
    def spread(held, at):
        return jnp.broadcast_to(held[:, at : at + 1], (8, 2 * eig_count))

    for step in range(0, eig_count, 2):
        at, group, inner = eig_count + step, step // 8, step % 8
        first = [spread(held, at) for held in groups[group:]]
        second = [spread(held, at + 1) for held in groups[group:]]
        upper = groups[group][inner : inner + 1, :]
        lower = groups[group][inner + 1 : inner + 2, :]
        top = 1.0 / first[0][inner : inner + 1, :]
        side = second[0][inner : inner + 1, :] * top
        cross = first[0][inner + 1 : inner + 2, :]
        lower = lower - cross * top * upper
        bottom = 1.0 / (second[0][inner + 1 : inner + 2, :] - cross * side)
        upper, lower = upper * top, lower * bottom
        for place in range(len(first)):
            one, two = first[place], second[place] - first[place] * side
            if place == 0:
                one, two = jnp.where(down > inner, one, 0.0), jnp.where(down > inner + 1, two, 0.0)
            groups[group + place] = groups[group + place] - one * upper - two * lower
    work = jnp.concatenate(groups, axis=0)
    pivots = jnp.sum(jnp.where(diagonal, work[:, eig_count:], 0.0), axis=1, keepdims=True)
    inverse = work[:, :eig_count] * lax.rsqrt(pivots)
    out_ref[...] = jnp.dot(
        inverse, smoothed, precision=lax.Precision.HIGHEST, preferred_element_type=jnp.float32
    )

    for item in FIRST_SENDS + sum(RELAYS.values(), ()):
        for copy in unit_copies(*item):
            copy.wait_send()
    for at in range(3):
        for piece in range(2):
            part_copy(at, piece).wait_send()


def per_device_full(total_rows, row_count, embeddings, vectors, block_pairs):
    del block_pairs
    eig_count, block_rows = vectors.shape
    near_rows, width = embeddings.shape
    col_count = near_rows // block_rows
    half = block_rows // 2
    padded = eig_count + 8
    dma = pltpu.SemaphoreType.DMA
    return pl.pallas_call(
        functools.partial(whole_kernel, total_rows),
        out_shape=jax.ShapeDtypeStruct((eig_count, block_rows), jnp.float32),
        in_specs=[pl.BlockSpec(memory_space=pl.ANY)] * 2,
        out_specs=pl.BlockSpec(memory_space=pltpu.VMEM),
        scratch_shapes=[
            pltpu.VMEM((near_rows, width), jnp.bfloat16),
            pltpu.VMEM((col_count, width, block_rows), jnp.bfloat16),
            pltpu.VMEM((eig_count, block_rows), jnp.bfloat16),
            pltpu.VMEM((UNITS, half, width), jnp.bfloat16),
            pltpu.VMEM((UNITS, eig_count, half), jnp.bfloat16),
            pltpu.VMEM((col_count, 8, block_rows), jnp.float32),
            pltpu.VMEM((col_count, padded, block_rows), jnp.float32),
            pltpu.VMEM((col_count - 1, padded, block_rows), jnp.float32),
            pltpu.VMEM((row_count, eig_count // 2, 2 * eig_count), jnp.float32),
            pltpu.VMEM((col_count, eig_count // 2, 2 * eig_count), jnp.float32),
            dma(()),
            dma(()),
            dma((2, UNITS)),
            dma((2, UNITS)),
            dma((UNITS,)),
            dma((UNITS,)),
            dma((2, col_count - 1)),
            dma((2, col_count - 1)),
            dma((row_count - 1,)),
            dma((row_count - 1,)),
            dma((col_count - 1,)),
            dma((col_count - 1,)),
        ],
        compiler_params=pltpu.CompilerParams(
            collective_id=0, has_side_effects=True, vmem_limit_bytes=60 * 1024 * 1024
        ),
    )(embeddings, vectors)


def solution(mesh):
    row_count, col_count = mesh.shape["row"], mesh.shape["col"]

    def step(embeddings, vectors, block_pairs):
        blocks = row_count * col_count
        full = block_pairs.shape[0] == blocks * (blocks - 1) and (row_count, col_count) == (8, 4)
        body = per_device
        if full:
            body = functools.partial(per_device_full, embeddings.shape[0], row_count)
        return jax.shard_map(
            body,
            mesh=mesh,
            in_specs=(P("row", None), P(None, ("row", "col")), P()),
            out_specs=P(None, ("row", "col")),
            check_vma=False,
        )(embeddings, vectors, block_pairs)

    return step
```

```python
import functools
import math

import jax
import jax.numpy as jnp
from jax import lax
from jax.experimental import pallas as pl
from jax.experimental.pallas import tpu as pltpu
from jax.sharding import PartitionSpec as P


def inverse_norms(blocks):
    return lax.rsqrt(jnp.mean(jnp.square(blocks.astype(jnp.float32)), axis=-1) + 1e-06)


def tile_terms(rows_x, cols_x, norm_rows, norm_cols, cols_v, feature_width):
    scores = jnp.dot(rows_x, cols_x.T, preferred_element_type=jnp.float32)
    affinity = jnp.exp(scores * norm_rows[:, None] * norm_cols[None, :] / math.sqrt(feature_width))
    rounded = affinity.astype(jnp.bfloat16)
    contrib = jnp.dot(cols_v, rounded.T, preferred_element_type=jnp.float32)
    return (contrib, jnp.sum(affinity, axis=1))


def tile_mask(block_pairs, near_column, col_count, row_count, here_row, here_col):
    near_ids = block_pairs[:, near_column]
    far_ids = block_pairs[:, 1 - near_column]
    member = (near_ids // col_count == here_row) & (far_ids % col_count == here_col)
    near_hot = ((near_ids % col_count)[:, None] == jnp.arange(col_count)[None, :]) & member[:, None]
    far_hot = (far_ids // col_count)[:, None] == jnp.arange(row_count)[None, :]
    return jnp.dot(
        near_hot.astype(jnp.float32).T,
        far_hot.astype(jnp.float32),
        preferred_element_type=jnp.float32,
    )


def add_block(running, contrib, row_totals, column_start, block_rows):
    sums_now, degree_now = running
    old_sums = lax.dynamic_slice_in_dim(sums_now, column_start, block_rows, 1)
    sums_now = lax.dynamic_update_slice_in_dim(sums_now, old_sums + contrib, column_start, 1)
    old_degree = lax.dynamic_slice_in_dim(degree_now, column_start, block_rows, 1)
    degree_now = lax.dynamic_update_slice_in_dim(
        degree_now, old_degree + row_totals[None, :], column_start, 1
    )
    return (sums_now, degree_now)


def per_device(embeddings, vectors, block_pairs):
    col_count = lax.axis_size("col")
    row_count = lax.axis_size("row")
    here_row = lax.axis_index("row")
    here_col = lax.axis_index("col")
    eig_count, block_rows = vectors.shape
    feature_width = embeddings.shape[1]
    near_blocks = embeddings.reshape(col_count, block_rows, feature_width)
    near_norms = inverse_norms(near_blocks)
    own_block = lax.dynamic_slice_in_dim(near_blocks, here_col, 1, 0)
    present = tile_mask(block_pairs, 0, col_count, row_count, here_row, here_col)
    start_sums = jnp.zeros((eig_count, col_count * block_rows), jnp.float32)
    start_degree = jnp.zeros((1, col_count * block_rows), jnp.float32)
    far_x = lax.all_gather(own_block, "row", axis=0, tiled=True)
    far_v = lax.all_gather(vectors[None], "row", axis=0, tiled=True)
    far_norms = inverse_norms(far_x)
    piece_blocks = far_x.shape[0]

    def visit(position, current):
        far_index = position // col_count
        near_index = position % col_count

        def compute(totals):
            contrib, row_totals = tile_terms(
                near_blocks[near_index],
                far_x[far_index],
                near_norms[near_index],
                far_norms[far_index],
                far_v[far_index],
                feature_width,
            )
            return add_block(totals, contrib, row_totals, near_index * block_rows, block_rows)

        return lax.cond(
            present[near_index, far_index] > 0.5, compute, lambda totals: totals, current
        )

    partial_sums, degree = lax.fori_loop(
        0, piece_blocks * col_count, visit, (start_sums, start_degree)
    )
    owned_sums, owned_degree = (
        lax.psum_scatter(partial_sums, "col", scatter_dimension=1, tiled=True),
        lax.psum_scatter(degree, "col", scatter_dimension=1, tiled=True),
    )
    smoothed = owned_sums / owned_degree
    total_rows = block_rows * col_count * row_count
    local_gram = jnp.dot(
        smoothed, smoothed.T, precision=lax.Precision.HIGHEST, preferred_element_type=jnp.float32
    )
    gram_matrix = lax.psum(local_gram, ("row", "col")) / total_rows
    factor = jnp.linalg.cholesky(gram_matrix)
    return lax.linalg.triangular_solve(factor, smoothed, left_side=True, lower=True)


UNITS = 16
FIRST_SENDS = ((0, 4, 2), (1, 5, 4), (0, 2, 1), (1, 3, 1), (1, 8, 2), (0, 9, 4))
RELAYS = {
    4: ((4, 12, 4), (5, 13, 2), (4, 6, 1), (5, 7, 1)),
    8: ((8, 10, 1), (9, 11, 1)),
    12: ((12, 14, 1), (13, 15, 1)),
}


def across(row, bits):
    if bits & 1:
        row = row + 1 - 2 * (row % 2)
    if bits & 2:
        row = row + 2 - 4 * ((row // 2) % 2)
    if bits & 4:
        row = row + 4 - 8 * ((row // 4) % 2)
    return row


def whole_kernel(
    total_rows,
    x_hbm,
    v_hbm,
    out_ref,
    own_x,
    turned_x,
    own_v,
    far_x,
    far_v,
    own_norm,
    acc,
    parts,
    plane_gram,
    depth_gram,
    own_sem,
    own_v_sem,
    x_send,
    x_recv,
    v_send,
    v_recv,
    part_send,
    part_recv,
    plane_send,
    plane_recv,
    depth_send,
    depth_recv,
):
    row = lax.axis_index("row")
    col = lax.axis_index("col")
    row_count = plane_gram.shape[0]
    col_count, padded, block_rows = acc.shape
    eig_count = own_v.shape[0]
    half = block_rows // 2
    quarter = half // 2
    width = own_x.shape[1]
    mesh_ids = pl.DeviceIdType.MESH

    load = pltpu.make_async_copy(x_hbm, own_x, own_sem)
    load.start()
    load_v = pltpu.make_async_copy(v_hbm, own_v, own_v_sem)
    load_v.start()

    barrier = pltpu.get_barrier_semaphore()
    for bits in range(1, row_count):
        pl.semaphore_signal(barrier, inc=1, device_id=(across(row, bits), col), device_id_type=mesh_ids)
    for step in range(1, col_count):
        pl.semaphore_signal(barrier, inc=1, device_id=(row, (col + step) % col_count), device_id_type=mesh_ids)
    pl.semaphore_wait(barrier, row_count + col_count - 2)

    def unit_copies(source, target, bits):
        if source < 2:
            start = pl.multiple_of(col * block_rows + source * half, half)
            x_src = [x_hbm.at[pl.ds(start + at * quarter, quarter), :] for at in range(2)]
            v_src = v_hbm.at[:, pl.ds(source * half, half)]
        else:
            x_src = [far_x.at[source, pl.ds(at * quarter, quarter), :] for at in range(2)]
            v_src = far_v.at[source]
        partner = (across(row, bits), col)
        return (
            pltpu.make_async_remote_copy(
                src_ref=v_src, dst_ref=far_v.at[target], send_sem=v_send.at[target],
                recv_sem=v_recv.at[target], device_id=partner, device_id_type=mesh_ids,
            ),
        ) + tuple(
            pltpu.make_async_remote_copy(
                src_ref=x_src[at], dst_ref=far_x.at[target, pl.ds(at * quarter, quarter), :],
                send_sem=x_send.at[at, target], recv_sem=x_recv.at[at, target],
                device_id=partner, device_id_type=mesh_ids,
            )
            for at in range(2)
        )

    def start_unit(item):
        for copy in unit_copies(*item):
            copy.start()

    def wait_v(target):
        pltpu.make_async_copy(far_v.at[target], far_v.at[target], v_recv.at[target]).wait()

    def wait_x(target, at):
        piece = far_x.at[target, pl.ds(at * quarter, quarter), :]
        pltpu.make_async_copy(piece, piece, x_recv.at[at, target]).wait()

    def wait_unit(target):
        wait_v(target)
        for at in range(2):
            wait_x(target, at)

    def relay(first):
        copies = [unit_copies(*item) for item in RELAYS[first]]
        wait_v(first)
        wait_v(first + 1)
        for held in copies:
            held[0].start()
        for at in range(2):
            wait_x(first, at)
            wait_x(first + 1, at)
            for held in copies:
                held[1 + at].start()

    for item in FIRST_SENDS:
        start_unit(item)

    load.wait()
    load_v.wait()
    far_v[0] = own_v[:, :half]
    far_v[1] = own_v[:, half:]
    for part in range(2):
        start = pl.multiple_of(col * block_rows + part * half, half)
        far_x[part] = own_x[pl.ds(start, half), :]
    acc[...] = jnp.zeros_like(acc)

    @pl.loop(0, col_count)
    def _(near):
        rows = own_x[pl.ds(pl.multiple_of(near * block_rows, block_rows), block_rows), :]
        turned = rows.astype(jnp.float32).T
        turned_x[near] = turned.astype(jnp.bfloat16)
        mean = jnp.sum(turned * turned, axis=0, keepdims=True) * (1.0 / width)
        own_norm[near] = jnp.broadcast_to(lax.rsqrt(mean + 1e-06), (8, block_rows))

    scale = 1.4426950408889634 / math.sqrt(width)

    def pair_norm(unit):
        wide = far_x[pl.ds(unit, 2)].reshape(block_rows, width).astype(jnp.float32)
        mean = jnp.sum(wide * wide, axis=1, keepdims=True) * (1.0 / width)
        return lax.rsqrt(mean + 1e-06) * scale

    def pair_scores(unit, near):
        cols = far_x[pl.ds(unit, 2)].reshape(block_rows, width)
        return jnp.dot(cols, turned_x[near], preferred_element_type=jnp.float32)

    def add_tile(unit, near, scores, col_norm):
        affinity = jnp.exp2(scores * own_norm[near, 0:1, :] * col_norm)
        acc[near, eig_count:, :] += jnp.sum(affinity.reshape(block_rows // 8, 8, block_rows), axis=0)
        cols_v = jnp.concatenate([far_v[unit], far_v[unit + 1]], axis=1)
        acc[near, :eig_count, :] += jnp.dot(
            cols_v, affinity.astype(jnp.bfloat16), preferred_element_type=jnp.float32
        )

    @pl.loop(0, UNITS // 2 - 2)
    def _(pair_at):
        unit = pair_at * 2

        @pl.when(unit == 2)
        def _():
            acc[col] = jnp.zeros((padded, block_rows), jnp.float32)

        for first in (4, 8):
            @pl.when(unit == first)
            def _(first=first):
                relay(first)

        for first in (2, 6, 10):
            @pl.when(unit == first)
            def _(first=first):
                wait_unit(first)
                wait_unit(first + 1)

        scores = pair_scores(unit, 0)
        col_norm = pair_norm(unit)
        for near in range(col_count):
            current = scores
            if near + 1 < col_count:
                scores = pair_scores(unit, near + 1)
            add_tile(unit, near, current, col_norm)

    pair = col + 1 - 2 * (col % 2)
    far = (col + 2) % col_count
    far_pair = col_count - 1 - col

    third = padded // 3
    pieces = tuple(pl.ds(start, third) for start in range(0, padded, third))

    def part_copy(at, piece):
        source, target = ((far_pair, pair), (pair, pair), (far, far))[at]
        rows = pieces[piece]
        return pltpu.make_async_remote_copy(
            src_ref=acc.at[source, rows, :], dst_ref=parts.at[at, rows, :],
            send_sem=part_send.at[piece, at], recv_sem=part_recv.at[piece, at],
            device_id=(row, target), device_id_type=mesh_ids,
        )

    last = UNITS - 2
    relay(last - 2)
    norms = {last - 2: pair_norm(last - 2)}

    def add_last(unit, near):
        add_tile(unit, near, pair_scores(unit, near), norms[unit])

    add_last(last - 2, far_pair)
    add_last(last - 2, pair)
    wait_unit(last)
    wait_unit(last + 1)
    norms[last] = pair_norm(last)
    add_last(last, far_pair)
    for piece in range(3):
        part_copy(0, piece).start()
    for near in (pair, far):
        add_last(last, near)
        if near is pair:
            add_last(last - 2, far)
    for piece, rows in enumerate(pieces):
        part_copy(0, piece).wait_recv()
        acc[far, rows, :] = acc[far, rows, :] + parts[0, rows, :]
        part_copy(2, piece).start()
        part_copy(1, piece).start()
    add_last(last - 2, col)
    add_last(last, col)
    for at in (1, 2):
        for piece in range(3):
            part_copy(at, piece).wait_recv()
    total = acc[col] + parts[1] + parts[2]
    degree = jnp.sum(total[eig_count:, :], axis=0, keepdims=True)
    smoothed = total[:eig_count, :] / degree

    def gram_sum(gram, held, me, partners, send_sem, recv_sem):
        held[me] = gram
        copies = []
        for at, partner in enumerate(partners):
            copies.append(
                pltpu.make_async_remote_copy(
                    src_ref=held.at[me], dst_ref=held.at[me], send_sem=send_sem.at[at],
                    recv_sem=recv_sem.at[at], device_id=partner, device_id_type=mesh_ids,
                )
            )
        for copy in copies:
            copy.start()
        for copy in copies:
            copy.wait()
        return jnp.sum(held[...], axis=0)

    gram = lax.dot_general(
        smoothed, smoothed, (((1,), (1,)), ((), ())),
        precision=lax.Precision.HIGHEST, preferred_element_type=jnp.float32,
    )
    packed = jnp.concatenate([gram[: eig_count // 2, :], gram[eig_count // 2 :, :]], axis=1)
    packed = gram_sum(
        packed, plane_gram, row, [(across(row, bits), col) for bits in range(1, row_count)],
        plane_send, plane_recv,
    )
    packed = gram_sum(
        packed, depth_gram, col, [(row, (col + step) % col_count) for step in range(1, col_count)],
        depth_send, depth_recv,
    )
    gram = jnp.concatenate([packed[:, :eig_count], packed[:, eig_count:]], axis=0) / total_rows

    down = lax.broadcasted_iota(jnp.int32, (8, 2 * eig_count), 0)
    at_row = lax.broadcasted_iota(jnp.int32, (eig_count, eig_count), 0)
    at_col = lax.broadcasted_iota(jnp.int32, (eig_count, eig_count), 1)
    diagonal = at_row == at_col
    work = jnp.concatenate([diagonal.astype(jnp.float32), gram], axis=1)
    groups = [work[start : start + 8, :] for start in range(0, eig_count, 8)]
    def spread(held, at):
        return jnp.broadcast_to(held[:, at : at + 1], (8, 2 * eig_count))

    for step in range(0, eig_count, 2):
        at, group, inner = eig_count + step, step // 8, step % 8
        first = [spread(held, at) for held in groups[group:]]
        second = [spread(held, at + 1) for held in groups[group:]]
        upper = groups[group][inner : inner + 1, :]
        lower = groups[group][inner + 1 : inner + 2, :]
        top = 1.0 / first[0][inner : inner + 1, :]
        side = second[0][inner : inner + 1, :] * top
        cross = first[0][inner + 1 : inner + 2, :]
        lower = lower - cross * top * upper
        bottom = 1.0 / (second[0][inner + 1 : inner + 2, :] - cross * side)
        upper, lower = upper * top, lower * bottom
        for place in range(len(first)):
            one, two = first[place], second[place] - first[place] * side
            if place == 0:
                one, two = jnp.where(down > inner, one, 0.0), jnp.where(down > inner + 1, two, 0.0)
            groups[group + place] = groups[group + place] - one * upper - two * lower
    work = jnp.concatenate(groups, axis=0)
    pivots = jnp.sum(jnp.where(diagonal, work[:, eig_count:], 0.0), axis=1, keepdims=True)
    inverse = work[:, :eig_count] * lax.rsqrt(pivots)
    out_ref[...] = jnp.dot(
        inverse, smoothed, precision=lax.Precision.HIGHEST, preferred_element_type=jnp.float32
    )

    for item in FIRST_SENDS + sum(RELAYS.values(), ()):
        for copy in unit_copies(*item):
            copy.wait_send()
    for at in range(3):
        for piece in range(3):
            part_copy(at, piece).wait_send()


def per_device_full(total_rows, row_count, embeddings, vectors, block_pairs):
    del block_pairs
    eig_count, block_rows = vectors.shape
    near_rows, width = embeddings.shape
    col_count = near_rows // block_rows
    half = block_rows // 2
    padded = eig_count + 8
    dma = pltpu.SemaphoreType.DMA
    return pl.pallas_call(
        functools.partial(whole_kernel, total_rows),
        out_shape=jax.ShapeDtypeStruct((eig_count, block_rows), jnp.float32),
        in_specs=[pl.BlockSpec(memory_space=pl.ANY)] * 2,
        out_specs=pl.BlockSpec(memory_space=pltpu.VMEM),
        scratch_shapes=[
            pltpu.VMEM((near_rows, width), jnp.bfloat16),
            pltpu.VMEM((col_count, width, block_rows), jnp.bfloat16),
            pltpu.VMEM((eig_count, block_rows), jnp.bfloat16),
            pltpu.VMEM((UNITS, half, width), jnp.bfloat16),
            pltpu.VMEM((UNITS, eig_count, half), jnp.bfloat16),
            pltpu.VMEM((col_count, 8, block_rows), jnp.float32),
            pltpu.VMEM((col_count, padded, block_rows), jnp.float32),
            pltpu.VMEM((col_count - 1, padded, block_rows), jnp.float32),
            pltpu.VMEM((row_count, eig_count // 2, 2 * eig_count), jnp.float32),
            pltpu.VMEM((col_count, eig_count // 2, 2 * eig_count), jnp.float32),
            dma(()),
            dma(()),
            dma((2, UNITS)),
            dma((2, UNITS)),
            dma((UNITS,)),
            dma((UNITS,)),
            dma((3, col_count - 1)),
            dma((3, col_count - 1)),
            dma((row_count - 1,)),
            dma((row_count - 1,)),
            dma((col_count - 1,)),
            dma((col_count - 1,)),
        ],
        compiler_params=pltpu.CompilerParams(
            collective_id=0, has_side_effects=True, vmem_limit_bytes=60 * 1024 * 1024
        ),
    )(embeddings, vectors)


def solution(mesh):
    row_count, col_count = mesh.shape["row"], mesh.shape["col"]

    def step(embeddings, vectors, block_pairs):
        blocks = row_count * col_count
        full = block_pairs.shape[0] == blocks * (blocks - 1) and (row_count, col_count) == (8, 4)
        body = per_device
        if full:
            body = functools.partial(per_device_full, embeddings.shape[0], row_count)
        return jax.shard_map(
            body,
            mesh=mesh,
            in_specs=(P("row", None), P(None, ("row", "col")), P()),
            out_specs=P(None, ("row", "col")),
            check_vma=False,
        )(embeddings, vectors, block_pairs)

    return step
```
